1024 devices in a mesh: expert: 16 (over z, y_lo), tensor: 64 (over x, y_hi, core).
Axes of the slice: x: 8, y: 8 (y_hi: 4, y_lo: 2; y = y_hi * 2 + y_lo), z: 8, core: 2. Of those that a mesh axis runs over, the one named last changes fastest.
Arguments:
- tokens: bfloat16 [6144, 2048], P('expert', 'tensor'), may hold values from -6 to 6
- cotangent: bfloat16 [6144, 2048], P('expert', 'tensor'), may hold values from -6 to 6
- routing: int32 [16, 384], P('expert'), may hold values from 0 to 383, each once within a row
- up_weight: bfloat16 [32, 2048, 4096], P('expert', None, 'tensor'), may hold values from -0.125 to 0.125
- down_weight: bfloat16 [32, 4096, 2048], P('expert', 'tensor'), may hold values from -0.09375 to 0.09375
- expert_embed: bfloat16 [32, 2048], P('expert'), may hold values from -0.125 to 0.125
Outputs:
- tokens_grad: bfloat16 [6144, 2048], P('expert', 'tensor')
- up_grad: bfloat16 [32, 2048, 4096], P('expert', None, 'tensor')
- down_grad: bfloat16 [32, 4096, 2048], P('expert', 'tensor')
- embed_grad: float32 [32, 2048], P('expert', 'tensor')
The draws below stay inside these ranges and needn't reach their ends.
Inputs may be any that keep to these rules, and one draw needn't show every extreme that they name: Each row of routing is a permutation of 0 .. 383; the entries at positions e * 12 .. (e + 1) * 12 - 1 are the tokens that this group assigns to expert e.
All inputs are finite; a program needn't handle non-finite values.
Results may differ from the reference program's by a relative error of at most 0.0075.
Values may be sent and summed in bfloat16 or wider, within the bound.
A program may use at most 32 MiB of HBM per device.

```python
import jax
import jax.numpy as jnp
from jax import lax

D = 2048
FF = 4096
SLOT = 12
SENDERS = 16
EXPERTS = 32
TOK_DEV = 384
TOKENS = 6144


def levels(stream_key, extent, cuts, least, largest):
    def one(position, parts):
        draws = jax.random.uniform(jax.random.fold_in(jax.random.fold_in(stream_key, 6), position), (parts,), jnp.float32, least / len(cuts), largest / len(cuts))
        return jnp.repeat(jnp.exp(draws), extent[position] // parts).reshape((-1,) + (1,) * (len(extent) - position - 1))

    loudness = one(*cuts[0])
    for cut in cuts[1:]:
        loudness = loudness * one(*cut)
    return loudness


def bell_draw(key, extent, spread, limit, pieces=(), dtype=jnp.bfloat16):
    gain = levels(key, extent, pieces, -0.22, 0.18) if pieces else 1.0
    drawn = jax.random.normal(key, extent, jnp.float32) * spread * gain
    return jnp.minimum(jnp.maximum(drawn, -limit), limit).astype(dtype)


def setup_inputs(seed: int = 0) -> dict:
    splits = jax.random.split(jax.random.key(seed), 7)
    return {
        "tokens": bell_draw(splits[0], (TOKENS, D), 1.0, 6.0, ((0, 16), (1, 64))),
        "cotangent": bell_draw(splits[1], (TOKENS, D), 1.0, 6.0, ((0, 16), (1, 64))),
        "routing": jax.vmap(lambda own: jax.random.permutation(own, TOK_DEV))(jax.random.split(splits[2], SENDERS)).reshape((SENDERS, TOK_DEV)).astype(jnp.int32),
        "up_weight": bell_draw(splits[3], (EXPERTS, D, FF), D ** -0.5, 0.125, ((0, 16), (2, 64))),
        "down_weight": bell_draw(splits[4], (EXPERTS, FF, D), FF ** -0.5, 0.09375, ((0, 16), (1, 64))),
        "expert_embed": bell_draw(splits[5], (EXPERTS, D), D ** -0.5, 0.125, ((0, 16),)),
    }


def expert_backward(inputs, upstream, up_w, down_w, emb_row):
    logits = jnp.dot(inputs, emb_row, preferred_element_type=jnp.float32)
    gating = jax.nn.sigmoid(logits)
    hidden = jnp.dot(inputs, up_w, preferred_element_type=jnp.float32)
    activated, pullback = jax.vjp(jax.nn.gelu, hidden)
    activated = activated.astype(jnp.bfloat16)
    back_raw = jnp.dot(upstream, down_w.T, preferred_element_type=jnp.float32)
    gate_total = lax.optimization_barrier(jnp.sum(activated.astype(jnp.float32) * back_raw, axis=1))
    slopes = gate_total * gating * (1.0 - gating)
    scaled = (gating[:, None] * upstream.astype(jnp.float32)).astype(jnp.bfloat16)
    down_grad = jnp.dot(activated.T, scaled, preferred_element_type=jnp.float32).astype(jnp.bfloat16)
    pre_grad, = pullback(gating[:, None] * back_raw)
    pre_grad = pre_grad.astype(jnp.bfloat16)
    up_grad = jnp.dot(inputs.T, pre_grad, preferred_element_type=jnp.float32).astype(jnp.bfloat16)
    input_grad = jnp.dot(pre_grad, up_w.T, preferred_element_type=jnp.float32)
    input_grad = (input_grad + slopes[:, None] * emb_row.astype(jnp.float32)).astype(jnp.bfloat16)
    embed_grad = lax.optimization_barrier(jnp.sum(slopes[:, None] * inputs.astype(jnp.float32), axis=0))
    return (input_grad, up_grad, down_grad, embed_grad)

def arrange(values, routing):
    grouped = values.reshape(SENDERS, TOK_DEV, D)
    picked = jax.vmap(lambda block, idx: jnp.take(block, idx, axis=0))(grouped, routing)
    picked = picked.reshape(SENDERS, EXPERTS, SLOT, D).transpose(1, 0, 2, 3)
    return picked.reshape(EXPERTS, SENDERS * SLOT, D)

def reference(tokens, cotangent, routing, up_weight, down_weight, expert_embed):
    inputs = arrange(tokens, routing)
    upstream = arrange(cotangent, routing)

    def one_expert(items):
        return expert_backward(items[0], items[1], items[2], items[3], items[4])
    input_grad, up_grad, down_grad, embed_grad = lax.map(one_expert, (inputs, upstream, up_weight, down_weight, expert_embed))
    ordered = input_grad.reshape(EXPERTS, SENDERS, SLOT, D).transpose(1, 0, 2, 3)
    ordered = ordered.reshape(SENDERS, TOK_DEV, D)
    placed = jax.vmap(lambda idx, block: jnp.zeros_like(block).at[idx].set(block))(routing, ordered)
    tokens_grad = (cotangent.astype(jnp.float32) + placed.reshape(TOKENS, D).astype(jnp.float32)).astype(jnp.bfloat16)
    return (tokens_grad, up_grad, down_grad, embed_grad)
```

```python
import functools

import jax
import jax.numpy as jnp
from jax import lax
from jax.experimental import pallas as pl
from jax.experimental.pallas import tpu as pltpu
from jax.sharding import PartitionSpec as P

Y = 4
KP = 16
BF = jnp.bfloat16
F32 = jnp.float32
NN = ((1,), (0,))
NT = ((1,), (1,))
TN = ((0,), (0,))


def dot(a, b, dims):
    return lax.dot_general(a, b, (dims, ((), ())), preferred_element_type=F32)


def remote(src, dst, ssem, rsem, device):
    return pltpu.make_async_remote_copy(
        src_ref=src,
        dst_ref=dst,
        send_sem=ssem,
        recv_sem=rsem,
        device_id=device,
        device_id_type=pl.DeviceIdType.MESH,
    )


def ones_where(hit):
    return hit.astype(F32).astype(BF)


def kernel(
    dims,
    tok_hbm, cot_hbm, rt_hbm, up_hbm, down_hbm, emb_hbm,
    tg_hbm, ug_hbm, dg_hbm, eg_hbm,
    both, rt, emb, ot, otq, bh, sbuf, rbuf, xg, w, u2, acc, l2, bd, gr,
    pf, outb, inb, vf, yo, yi, gp, gy, gs, gx, ego, egi, egv, tgv, sbuf2, rbuf2,
    lsem, osem,
    w_s, w_r, a_s, a_r, y_s, y_r, ring_s, ring_r, ch_s, ch_r, yr_s, yr_r,
    gy_s, gy_r, gx_s, gx_r, g_s, g_r, e_s, e_r, b_s, b_r,
):
    NE, SL, CW, X, FL = dims
    H = X // 2
    HR = NE * SL
    R = 2 * HR
    NQ = NE * KP
    CF = 2 * FL
    SW = Y * 2 * CW
    CH = 2 * CW
    PW = Y * CW
    D = X * SW
    e = lax.axis_index("expert")
    t = lax.axis_index("tensor")
    core = lax.rem(t, 2)
    chip = t // 2
    y = lax.rem(chip, Y)
    x = chip // Y
    other = 1 - core

    def xa(d):
        return lax.rem(x + (d + X), X)

    def ya(d):
        return lax.rem(y + (d + Y), Y)

    def ea(d):
        return lax.rem(e + (d + NE), NE)

    def tid(xx, yy, cc):
        return (xx * Y + yy) * 2 + cc

    sib = (e, tid(x, y, other))
    sends = []

    def go(src, dst, ssem, rsem, device):
        copy = remote(src, dst, ssem, rsem, device)
        copy.start()
        sends.append(copy)

    def drain():
        for copy in sends:
            copy.wait_send()
        sends.clear()

    def got(dst, ssem, rsem):
        remote(dst, dst, ssem, rsem, sib).wait_recv()

    barrier = pltpu.get_barrier_semaphore()
    pairs = [(rel, o) for o in range(NE) for rel in range(2) if rel or o]
    peers = [(ea(o), tid(x, y, core if rel == 0 else other)) for rel, o in pairs]
    peers += [(e, tid(x, ya(dy), core)) for dy in range(1, Y)]
    peers += [(e, tid(xa(dx), y, core)) for dx in range(1, X)]
    for peer in peers:
        pl.semaphore_signal(barrier, inc=1, device_id=peer, device_id_type=pl.DeviceIdType.MESH)

    loads = [
        pltpu.make_async_copy(rt_hbm, rt, lsem.at[0]),
        pltpu.make_async_copy(tok_hbm, both.at[pl.ds(0, CW)], lsem.at[1]),
        pltpu.make_async_copy(cot_hbm, both.at[pl.ds(CW, CW)], lsem.at[2]),
        pltpu.make_async_copy(emb_hbm, emb, lsem.at[3]),
        pltpu.make_async_copy(
            up_hbm.at[pl.ds(pl.multiple_of(core * FL, FL), FL)],
            w.at[pl.ds(pl.multiple_of(core * FL, FL), FL)],
            lsem.at[4],
        ),
        pltpu.make_async_copy(
            down_hbm.at[pl.ds(pl.multiple_of(core * FL, FL), FL)],
            w.at[pl.ds(pl.multiple_of(CF + core * FL, FL), FL)],
            lsem.at[5],
        ),
    ]
    for copy in loads:
        copy.start()

    qrow = lax.broadcasted_iota(jnp.int32, (NQ, R), 0)
    qcol = lax.broadcasted_iota(jnp.int32, (NQ, R), 1)
    qg = lax.shift_right_logical(qrow, 4)
    qk = lax.bitwise_and(qrow, KP - 1)

    def by_expert(el):
        return ones_where((qcol == qg * (2 * SL) + el * SL + qk) & (qk < SL))

    def by_half(half):
        return ones_where((qcol == half * HR + qg * SL + qk) & (qk < SL))

    acc[...] = jnp.zeros_like(acc)
    for c in range(2):
        bh[c] = by_half(c)
    for copy in loads[:3]:
        copy.wait()
    tok_of = lax.broadcasted_iota(jnp.int32, (R, R), 0)
    ot[...] = ones_where(tok_of == rt[...])
    ordered = dot(both[...], ot[...], NN).astype(BF)
    pad = jnp.zeros((NQ, 64), BF)
    for el in range(2):
        block = dot(by_expert(el), ordered, NT).astype(BF)
        sbuf[el] = jnp.concatenate([block, pad], axis=1).reshape(NE, KP, CH + 64)
    pl.semaphore_wait(barrier, len(peers))

    for rel, o in sorted(pairs, key=lambda p: -min(p[1], NE - p[1])):
        to = core if rel == 0 else other
        k = rel * NE + o
        go(sbuf.at[to, ea(o)], rbuf.at[core, e], a_s.at[k], a_r.at[k], (ea(o), tid(x, y, to)))
    rbuf[core, e] = sbuf[core, e]
    mine = pl.ds(pl.multiple_of(core * FL, FL), FL)
    mine_dn = pl.ds(pl.multiple_of(CF + core * FL, FL), FL)
    his = pl.ds(pl.multiple_of(other * FL, FL), FL)
    his_dn = pl.ds(pl.multiple_of(CF + other * FL, FL), FL)
    go(up_hbm.at[his], w.at[mine], w_s.at[0], w_r.at[0], sib)
    go(down_hbm.at[his], w.at[mine_dn], w_s.at[1], w_r.at[1], sib)
    for rel, o in pairs:
        k = rel * NE + o
        got(rbuf.at[core if rel == 0 else other, ea(-o)], a_s.at[k], a_r.at[k])
    for c in range(2):
        landed = rbuf[c].reshape(NQ, CH + 64)
        part = dot(landed[:, :CW], bh[0], TN) + dot(landed[:, CW:CH], bh[1], TN)
        xg[pl.ds(pl.multiple_of(chip * CH + c * CW, CW), CW), :] = part.astype(BF)

    def chunk(xx, yy):
        return xg.at[pl.ds(pl.multiple_of((xx * Y + yy) * CH, CH), CH)]

    order = [0] + sorted(range(1, Y), key=lambda d: min(d, Y - d))
    halves = (set(range(Y // 2)), set(range(Y // 2, Y)))

    def slot(direction, step, j):
        return (direction * (H + 1) + step) * Y + j

    def onward(direction, step, j, piece):
        to = (e, tid(xa(1 if direction == 0 else -1), y, core))
        k = slot(direction, step, j)
        go(piece, piece, ring_s.at[k], ring_r.at[k], to)

    own = chunk(x, y)
    onward(0, 1, 0, own)
    onward(1, 1, 0, own)
    for dy in reversed(order[1:]):
        go(own, own, y_s.at[dy], y_r.at[dy], (e, tid(x, ya(dy), core)))

    drain()
    for copy in loads[3:]:
        copy.wait()
    got(w.at[his], w_s.at[0], w_r.at[0])
    got(w.at[his_dn], w_s.at[1], w_r.at[1])
    erow = lax.broadcasted_iota(jnp.int32, (KP, D), 0)
    both_emb = emb[...].astype(F32)
    own_emb = jnp.where(core == 0, both_emb[0:1], both_emb[1:2])
    w[pl.ds(2 * CF, KP), :] = jnp.where(erow == 0, own_emb, 0.0).astype(BF)

    def spread(xx):
        at = pl.ds(xx * SW, SW)
        srow = lax.broadcasted_iota(jnp.int32, (SW, PW), 0)
        scol = lax.broadcasted_iota(jnp.int32, (SW, PW), 1)
        src = (scol // CW) * CH + lax.rem(scol, CW)
        for c in range(2):
            pick = ones_where(srow == src + c * CW)
            u2[pl.ds(c * CF, CF), pl.ds(xx * PW, PW)] = dot(w[pl.ds(0, CF), at], pick, NN).astype(BF)

    def use(xx):
        at = pl.ds(pl.multiple_of(xx * SW, SW), SW)
        acc[...] += dot(w[:, at], xg[at, :], NN)

    for j, dy in enumerate(order):
        if dy:
            piece = chunk(x, ya(-dy))
            got(piece, y_s.at[dy], y_r.at[dy])
            onward(0, 1, j, piece)
            onward(1, 1, j, piece)
    use(x)
    for step in range(1, H + 1):
        for j, dy in enumerate(order):
            for direction in range(2):
                if step == H and j not in halves[direction]:
                    continue
                piece = chunk(xa(-step if direction == 0 else step), ya(-dy))
                k = slot(direction, step, j)
                got(piece, ring_s.at[k], ring_r.at[k])
                if step < H - 1 or (step == H - 1 and j in halves[direction]):
                    onward(direction, step + 1, j, piece)
        if step < H:
            use(xa(-step))
            use(xa(step))
            for k in range((step - 1) * X // (H - 1), step * X // (H - 1)):
                spread(k)
    use(xa(H))

    lane = lax.broadcasted_iota(jnp.int32, (1, R), 1)
    lo = lane < HR

    def doubled(v, half):
        turned = pltpu.roll(v, HR, 1)
        return jnp.where(lo, v, turned) if half == 0 else jnp.where(lo, turned, v)

    hidden = doubled(acc[pl.ds(0, CF), :], 0)
    back = doubled(acc[pl.ds(CF, CF), :], 1)
    logit = doubled(acc[pl.ds(2 * CF, 8), :], 0)[0:1]
    gating = 1.0 / (1.0 + jnp.exp(-logit))
    c0 = 0.7978845608028654
    c1 = 0.044715
    sq = hidden * hidden
    th = jnp.tanh(c0 * (hidden + c1 * (sq * hidden)))
    cdf = 0.5 * (1.0 + th)
    act = hidden * cdf
    slope = cdf + (0.5 * hidden) * (1.0 - th * th) * (c0 * (1.0 + (3.0 * c1) * sq))
    zero = jnp.zeros_like(hidden)
    pre = slope * (gating * back)
    pre_lo = jnp.where(lo, pre, zero).astype(BF)
    bd[pl.ds(0, CF), :] = pre_lo
    bd[pl.ds(CF, CF), :] = jnp.where(lo, zero, pre).astype(BF)

    def partial(d):
        xx = xa(d)
        at = pl.ds(pl.multiple_of(xx * PW, PW), PW)
        pf[xx] = dot(u2[:, at], bd[...], TN).reshape(Y, CW, R)

    ahead = sorted(range(Y), key=lambda d: -min(d, Y - d))

    def pass_on(direction, m, j):
        to = (e, tid(xa(1 if direction == 0 else -1), y, core))
        k = slot(direction, m, j)
        go(outb.at[direction, m, j], inb.at[direction, m, j], ch_s.at[k], ch_r.at[k], to)

    def came(direction, m, j):
        k = slot(direction, m, j)
        got(inb.at[direction, m, j], ch_s.at[k], ch_r.at[k])
        return inb[direction, m, j].astype(F32)

    partial(H)
    for j in range(Y):
        direction = 0 if j in halves[0] else 1
        outb[direction, 1, j] = pf[xa(H), ya(ahead[j])].astype(BF)
        pass_on(direction, 1, j)

    l2[pl.ds(0, CF), :] = pre_lo
    l2[pl.ds(CF, CF), :] = jnp.where(lo, zero, act * gating).astype(BF)
    gp[...] = jnp.sum(act.astype(BF).astype(F32) * back, axis=0, keepdims=True)
    for dy in range(1, Y):
        go(gp, gy.at[dy], gy_s.at[dy], gy_r.at[dy], (e, tid(x, ya(dy), core)))
    def grads(k):
        at = pl.ds(k * SW, SW)
        gr[:, at] = dot(l2[...], xg[at, :], NT).astype(BF)

    done = 0
    for m in range(2, H + 1):
        if m == 2:
            partial(H - 1)
            partial(1 - H)
        for first_part in (True, False):
            if m == 2 and not first_part:
                for d in range(H - 2, 0, -1):
                    partial(d)
                    partial(-d)
                partial(0)
            for j in range(Y):
                for direction in range(2):
                    late = j in halves[direction]
                    if late == first_part:
                        continue
                    dest = xa((H + 1 - m) * (1 if direction == 0 else -1))
                    value = pf[dest, ya(ahead[j])]
                    if m > 2 or late:
                        value = value + came(direction, m - 1, j)
                    outb[direction, m, j] = value.astype(BF)
                    pass_on(direction, m, j)
        drain()
        if m == 2:
            total = gp[...]
            for dy in range(1, Y):
                got(gy.at[dy], gy_s.at[dy], gy_r.at[dy])
                total = total + gy[dy]
            gs[...] = total
            for dx in range(1, X):
                go(gs, gx.at[dx], gx_s.at[dx], gx_r.at[dx], (e, tid(xa(dx), y, core)))
        for _ in range(X // (H - 1)):
            grads(done)
            done += 1
    while done < X:
        grads(done)
        done += 1
    outs = [
        pltpu.make_async_copy(gr.at[mine], ug_hbm.at[mine], osem.at[0]),
        pltpu.make_async_copy(gr.at[mine_dn], dg_hbm.at[mine], osem.at[1]),
    ]
    for copy in outs:
        copy.start()
    go(gr.at[his], ug_hbm.at[mine], g_s.at[0], g_r.at[0], sib)
    go(gr.at[his_dn], dg_hbm.at[mine], g_s.at[1], g_r.at[1], sib)

    gate_total = gs[...]
    for dx in range(1, X):
        got(gx.at[dx], gx_s.at[dx], gx_r.at[dx])
        gate_total = gate_total + gx[dx]
    slopes = gate_total * gating * (1.0 - gating)
    srow = lax.broadcasted_iota(jnp.int32, (KP, R), 0)
    one_row = jnp.where((srow == 0) & lo, slopes, 0.0)
    hi = one_row.astype(BF)
    rest = one_row - hi.astype(F32)
    mid = rest.astype(BF)
    low = (rest - mid.astype(F32)).astype(BF)

    def embed_part(tt):
        xs = xg[pl.ds(pl.multiple_of(tt * CW, CW), CW), :]
        return (dot(hi, xs, NT) + dot(mid, xs, NT) + dot(low, xs, NT))[0:8]

    ego[...] = jnp.concatenate(
        [embed_part(tid(x, y, other)), jnp.zeros((8, 128 - CW), F32)], axis=1
    )
    go(ego, egi, e_s.at[0], e_r.at[0], sib)
    own_part = embed_part(t)[0:1]
    prow = lax.broadcasted_iota(jnp.int32, (CW, D), 0)
    pcol = lax.broadcasted_iota(jnp.int32, (CW, D), 1)
    erows = w[pl.ds(2 * CF, KP), :]
    ecol = [
        dot(ones_where(pcol == prow + (chip * CH + c * CW)), erows, NT)[:, 0:1] for c in range(2)
    ]
    outer = jnp.where(lo, ecol[0], ecol[1]) * slopes
    for el in range(2):
        otq[el] = dot(by_expert(el), ot[...], NT).astype(BF)

    for j in range(Y):
        dy = ahead[j]
        value = pf[x, ya(dy)] + came(0, H, j) + came(1, H, j)
        if dy:
            yo[dy] = value.astype(BF)
            go(yo.at[dy], yi.at[dy], yr_s.at[dy], yr_r.at[dy], (e, tid(x, ya(dy), core)))
        else:
            summed = value + outer
    drain()
    for dy in sorted(range(1, Y), key=lambda d: min(d, Y - d)):
        got(yi.at[dy], yr_s.at[dy], yr_r.at[dy])
        summed = summed + yi[dy].astype(F32)
    summed = summed.astype(BF)

    pad = jnp.zeros((NQ, 128 - CW), BF)
    for c in range(2):
        block = dot(bh[c], summed, NT).astype(BF)
        sbuf2[c] = jnp.concatenate([block, pad], axis=1).reshape(NE, KP, 128)
    for rel, o in sorted(pairs, key=lambda p: -min(p[1], NE - p[1])):
        to = core if rel == 0 else other
        k = rel * NE + o
        go(sbuf2.at[to, ea(o)], rbuf2.at[core, e], b_s.at[k], b_r.at[k], (ea(o), tid(x, y, to)))
    rbuf2[core, e] = sbuf2[core, e]
    drain()
    got(egi, e_s.at[0], e_r.at[0])
    row2 = lax.broadcasted_iota(jnp.int32, (2, CW), 0)
    egv[...] = jnp.where(row2 == core, own_part, egi[...][0:1, :CW])
    outs.append(pltpu.make_async_copy(egv, eg_hbm, osem.at[2]))
    outs[-1].start()
    got(ug_hbm.at[his], g_s.at[0], g_r.at[0])
    got(dg_hbm.at[his], g_s.at[1], g_r.at[1])
    for rel, o in pairs:
        k = rel * NE + o
        got(rbuf2.at[core if rel == 0 else other, ea(-o)], b_s.at[k], b_r.at[k])
    placed = sum(dot(rbuf2[el].reshape(NQ, 128)[:, :CW], otq[el], TN) for el in range(2))
    tgv[...] = (both[pl.ds(CW, CW), :].astype(F32) + placed).astype(BF)
    outs.append(pltpu.make_async_copy(tgv, tg_hbm, osem.at[3]))
    outs[-1].start()
    for copy in outs:
        copy.wait()


def hand_over(*refs):
    ins, outs, held, sems = refs[:4], refs[4:8], refs[8:12], refs[12]
    first = [pltpu.make_async_copy(ins[i], held[i], sems.at[i]) for i in range(4)]
    second = [pltpu.make_async_copy(held[i], outs[i], sems.at[4 + i]) for i in range(4)]
    for copy in first:
        copy.start()
    for i in range(4):
        first[i].wait()
        second[i].start()
    for copy in second:
        copy.wait()


def local(groups, tensors, tokens, cotangent, routing, up_weight, down_weight, expert_embed):
    rows, cw = tokens.shape
    el, depth, fl = up_weight.shape
    sl = rows // (groups * el)
    xs = tensors // (2 * Y)
    dims = (groups, sl, cw, xs, fl)
    h = xs // 2
    cf = 2 * fl
    vm = pltpu.VMEM
    dma = pltpu.SemaphoreType.DMA
    n_ring = 2 * (h + 1) * Y

    def pair(n):
        return [dma((n,)), dma((n,))]

    scratch = [
        vm((2 * cw, rows), BF),
        vm((1, rows), jnp.int32),
        vm((el, depth), BF),
        vm((rows, rows), BF),
        vm((2, groups * KP, rows), BF),
        vm((2, groups * KP, rows), BF),
        vm((2, groups, KP, 2 * cw + 64), BF),
        vm((2, groups, KP, 2 * cw + 64), BF),
        vm((depth, rows), BF),
        vm((2 * cf + KP, depth), BF),
        vm((2 * cf, depth // 2), BF),
        vm((2 * cf + KP, rows), F32),
        vm((2 * cf, rows), BF),
        vm((2 * cf, rows), BF),
        vm((2 * cf, depth), BF),
        vm((xs, Y, cw, rows), F32),
        vm((2, h + 1, Y, cw, rows), BF),
        vm((2, h + 1, Y, cw, rows), BF),
        vm((Y, cw, rows), F32),
        vm((Y, cw, rows), BF),
        vm((Y, cw, rows), BF),
        vm((1, rows), F32),
        vm((Y, 1, rows), F32),
        vm((1, rows), F32),
        vm((xs, 1, rows), F32),
        vm((8, 128), F32),
        vm((8, 128), F32),
        vm((el, cw), F32),
        vm((cw, rows), BF),
        vm((2, groups, KP, 128), BF),
        vm((2, groups, KP, 128), BF),
        dma((6,)),
        dma((4,)),
        *pair(2),
        *pair(2 * groups),
        *pair(Y),
        *pair(n_ring),
        *pair(n_ring),
        *pair(Y),
        *pair(Y),
        *pair(xs),
        *pair(2),
        *pair(1),
        *pair(2 * groups),
    ]
    hbm = pl.BlockSpec(memory_space=pl.ANY)
    shapes = (
        jax.ShapeDtypeStruct((cw, rows), BF),
        jax.ShapeDtypeStruct((el * fl, depth), BF),
        jax.ShapeDtypeStruct((el * fl, depth), BF),
        jax.ShapeDtypeStruct((el, cw), F32),
    )
    made = pl.pallas_call(
        functools.partial(kernel, dims),
        out_shape=shapes,
        in_specs=[hbm] * 6,
        out_specs=(hbm,) * 4,
        scratch_shapes=scratch,
        compiler_params=pltpu.CompilerParams(
            collective_id=0, has_side_effects=True, vmem_limit_bytes=60 * 1024 * 1024
        ),
    )(
        tokens.T,
        cotangent.T,
        routing,
        up_weight.transpose(0, 2, 1).reshape(el * fl, depth),
        down_weight.reshape(el * fl, depth),
        expert_embed,
    )
    tg, ug, dg, eg = pl.pallas_call(
        hand_over,
        out_shape=shapes,
        in_specs=[hbm] * 4,
        out_specs=(hbm,) * 4,
        scratch_shapes=[vm(shape.shape, shape.dtype) for shape in shapes] + [dma((8,))],
        compiler_params=pltpu.CompilerParams(vmem_limit_bytes=60 * 1024 * 1024),
    )(*made)
    return (
        tg.T,
        ug.reshape(el, fl, depth).transpose(0, 2, 1),
        dg.reshape(el, fl, depth),
        eg,
    )


def solution(mesh):
    return jax.shard_map(
        functools.partial(local, mesh.shape["expert"], mesh.shape["tensor"]),
        mesh=mesh,
        in_specs=(
            P("expert", "tensor"),
            P("expert", "tensor"),
            P("expert", None),
            P("expert", None, "tensor"),
            P("expert", "tensor", None),
            P("expert", None),
        ),
        out_specs=(
            P("expert", "tensor"),
            P("expert", None, "tensor"),
            P("expert", "tensor", None),
            P("expert", "tensor"),
        ),
        check_vma=False,
    )
```

```python
import functools

import jax
import jax.numpy as jnp
from jax import lax
from jax.experimental import pallas as pl
from jax.experimental.pallas import tpu as pltpu
from jax.sharding import PartitionSpec as P

Y = 4
KP = 16
BF = jnp.bfloat16
F32 = jnp.float32
NN = ((1,), (0,))
NT = ((1,), (1,))
TN = ((0,), (0,))


def dot(a, b, dims):
    return lax.dot_general(a, b, (dims, ((), ())), preferred_element_type=F32)


def remote(src, dst, ssem, rsem, device):
    return pltpu.make_async_remote_copy(
        src_ref=src,
        dst_ref=dst,
        send_sem=ssem,
        recv_sem=rsem,
        device_id=device,
        device_id_type=pl.DeviceIdType.MESH,
    )


def ones_where(hit):
    return hit.astype(F32).astype(BF)


def kernel(
    dims,
    tok_hbm, cot_hbm, rt_hbm, up_hbm, down_hbm, emb_hbm,
    tg_hbm, ug_hbm, dg_hbm, eg_hbm,
    both, rt, emb, ot, otq, bh, sbuf, rbuf, xg, w, u2, acc, l2, bd, gr,
    pf, outb, inb, yo, yi, gp, gy, gs, gx, ego, egi, egv, tgv, sbuf2, rbuf2,
    lsem, osem,
    w_s, w_r, a_s, a_r, y_s, y_r, ring_s, ring_r, ch_s, ch_r, yr_s, yr_r,
    gy_s, gy_r, gx_s, gx_r, g_s, g_r, e_s, e_r, b_s, b_r,
):
    NE, SL, CW, X, FL = dims
    H = X // 2
    HR = NE * SL
    R = 2 * HR
    NQ = NE * KP
    CF = 2 * FL
    SW = Y * 2 * CW
    CH = 2 * CW
    PW = Y * CW
    D = X * SW
    e = lax.axis_index("expert")
    t = lax.axis_index("tensor")
    core = lax.rem(t, 2)
    chip = t // 2
    y = lax.rem(chip, Y)
    x = chip // Y
    other = 1 - core

    def xa(d):
        return lax.rem(x + (d + X), X)

    def ya(d):
        return lax.rem(y + (d + Y), Y)

    def ea(d):
        return lax.rem(e + (d + NE), NE)

    def tid(xx, yy, cc):
        return (xx * Y + yy) * 2 + cc

    sib = (e, tid(x, y, other))
    sends = []

    def go(src, dst, ssem, rsem, device, single=True):
        copy = remote(src, dst, ssem, rsem, device)
        copy.start()
        if single:
            sends.append(copy)

    def gone(src, ssem, rsem):
        remote(src, src, ssem, rsem, sib).wait_send()

    def drain():
        for copy in sends:
            copy.wait_send()
        sends.clear()

    def got(dst, ssem, rsem):
        remote(dst, dst, ssem, rsem, sib).wait_recv()

    barrier = pltpu.get_barrier_semaphore()
    pairs = [(rel, o) for o in range(NE) for rel in range(2) if rel or o]
    pairs.sort(key=lambda p: -min(p[1], NE - p[1]))
    peers = [(ea(o), tid(x, y, core if rel == 0 else other)) for rel, o in pairs]
    peers += [(e, tid(x, ya(dy), core)) for dy in range(1, Y)]
    peers += [(e, tid(xa(dx), y, core)) for dx in range(1, X)]
    loads = [
        pltpu.make_async_copy(rt_hbm, rt, lsem.at[0]),
        pltpu.make_async_copy(tok_hbm, both.at[pl.ds(0, CW)], lsem.at[1]),
        pltpu.make_async_copy(cot_hbm, both.at[pl.ds(CW, CW)], lsem.at[2]),
        pltpu.make_async_copy(emb_hbm, emb, lsem.at[3]),
        pltpu.make_async_copy(
            up_hbm.at[pl.ds(pl.multiple_of(core * FL, FL), FL)],
            w.at[pl.ds(pl.multiple_of(core * FL, FL), FL)],
            lsem.at[4],
        ),
        pltpu.make_async_copy(
            down_hbm.at[pl.ds(pl.multiple_of(core * FL, FL), FL)],
            w.at[pl.ds(pl.multiple_of(CF + core * FL, FL), FL)],
            lsem.at[5],
        ),
    ]
    for copy in loads[:3]:
        copy.start()
    for peer in peers:
        pl.semaphore_signal(barrier, inc=1, device_id=peer, device_id_type=pl.DeviceIdType.MESH)
    for copy in loads[3:]:
        copy.start()

    qrow = lax.broadcasted_iota(jnp.int32, (NQ, R), 0)
    qcol = lax.broadcasted_iota(jnp.int32, (NQ, R), 1)
    qg = lax.shift_right_logical(qrow, 4)
    qk = lax.bitwise_and(qrow, KP - 1)

    def by_expert(el):
        return ones_where((qcol == qg * (2 * SL) + el * SL + qk) & (qk < SL))

    def by_half(half):
        return ones_where((qcol == half * HR + qg * SL + qk) & (qk < SL))

    for copy in loads[:3]:
        copy.wait()
    tok_of = lax.broadcasted_iota(jnp.int32, (R, R), 0)
    ot[...] = ones_where(tok_of == rt[...])
    ordered = dot(both[...], ot[...], NN).astype(BF)
    pad = jnp.zeros((NQ, 64), BF)
    for el in range(2):
        block = dot(by_expert(el), ordered, NT).astype(BF)
        sbuf[pl.ds(el * NE, NE)] = jnp.concatenate([block, pad], axis=1).reshape(NE, KP, CH + 64)
    pl.semaphore_wait(barrier, len(peers))

    for rel, o in pairs:
        to = core if rel == 0 else other
        go(
            sbuf.at[to * NE + ea(o)], rbuf.at[core * NE + e],
            a_s.at[0], a_r.at[0], (ea(o), tid(x, y, to)), False,
        )
    rbuf[core * NE + e] = sbuf[core * NE + e]
    mine = pl.ds(pl.multiple_of(core * FL, FL), FL)
    mine_dn = pl.ds(pl.multiple_of(CF + core * FL, FL), FL)
    his = pl.ds(pl.multiple_of(other * FL, FL), FL)
    his_dn = pl.ds(pl.multiple_of(CF + other * FL, FL), FL)
    go(up_hbm.at[his], w.at[mine], w_s.at[0], w_r.at[0], sib)
    go(down_hbm.at[his], w.at[mine_dn], w_s.at[1], w_r.at[1], sib)
    acc[...] = jnp.zeros_like(acc)
    for c in range(2):
        bh[c] = by_half(c)
    got(rbuf.at[pl.ds(0, 2 * NE - 1)], a_s.at[0], a_r.at[0])
    for c in range(2):
        landed = rbuf[pl.ds(c * NE, NE)].reshape(NQ, CH + 64)
        part = dot(landed[:, :CW], bh[0], TN) + dot(landed[:, CW:CH], bh[1], TN)
        xg[pl.ds(pl.multiple_of(chip * CH + c * CW, CW), CW), :] = part.astype(BF)

    def chunk(xx, yy, half):
        return xg.at[pl.ds(pl.multiple_of((xx * Y + yy) * CH + half * CW, CW), CW)]

    near = sorted(range(1, Y), key=lambda d: min(d, Y - d))
    beside = [dy for dy in near if min(dy, Y - dy) == 1]
    beyond = [dy for dy in near if min(dy, Y - dy) > 1]
    order = [(0, 0), (0, 1)]
    order += [(dy, half) for group in (beside, beyond) for half in range(2) for dy in group]
    NJ = len(order)

    def gslot(direction, step, j):
        return (direction * (H + 1) + step) * NJ + j

    halves = (set(range(Y // 2)), set(range(Y // 2, Y)))

    def slot(direction, step, j):
        return (direction * (H + 1) + step) * Y + j

    def onward(direction, step, j, piece):
        to = (e, tid(xa(1 if direction == 0 else -1), y, core))
        k = gslot(direction, step, j)
        go(piece, piece, ring_s.at[0], ring_r.at[k], to, False)

    for j in range(2):
        for direction in range(2):
            onward(direction, 1, j, chunk(x, y, j))
    for dy, half in order[2:]:
        own = chunk(x, y, half)
        k = dy * 2 + half
        go(own, own, y_s.at[k], y_r.at[k], (e, tid(x, ya(dy), core)))

    drain()
    gone(sbuf.at[pl.ds(0, 2 * NE - 1)], a_s.at[0], a_r.at[0])
    for copy in loads[3:]:
        copy.wait()
    got(w.at[his], w_s.at[0], w_r.at[0])
    got(w.at[his_dn], w_s.at[1], w_r.at[1])
    erow = lax.broadcasted_iota(jnp.int32, (KP, D), 0)
    both_emb = emb[...].astype(F32)
    own_emb = jnp.where(core == 0, both_emb[0:1], both_emb[1:2])
    w[pl.ds(2 * CF, KP), :] = jnp.where(erow == 0, own_emb, 0.0).astype(BF)

    def spread(xx):
        at = pl.ds(xx * SW, SW)
        srow = lax.broadcasted_iota(jnp.int32, (SW, PW), 0)
        scol = lax.broadcasted_iota(jnp.int32, (SW, PW), 1)
        src = (scol // CW) * CH + lax.rem(scol, CW)
        for c in range(2):
            pick = ones_where(srow == src + c * CW)
            u2[pl.ds(c * CF, CF), pl.ds(xx * PW, PW)] = dot(w[pl.ds(0, CF), at], pick, NN).astype(BF)

    def use(xx):
        at = pl.ds(pl.multiple_of(xx * SW, SW), SW)
        acc[...] += dot(w[:, at], xg[at, :], NN)

    def relay(step, j):
        dy, half = order[j]
        for direction in range(2):
            if step == H and half != direction:
                continue
            piece = chunk(xa(-step if direction == 0 else step), ya(-dy), half)
            got(piece, ring_s.at[0], ring_r.at[gslot(direction, step, j)])
            if step < H - 1 or (step == H - 1 and half == direction):
                onward(direction, step + 1, j, piece)

    def beginning(j):
        dy, half = order[j]
        piece = chunk(x, ya(-dy), half)
        k = dy * 2 + half
        got(piece, y_s.at[k], y_r.at[k])
        onward(0, 1, j, piece)
        onward(1, 1, j, piece)

    lead = 2 + len(beside)
    for j in range(2, lead):
        beginning(j)
    relay(1, 0)
    relay(1, 1)
    for j in range(lead, NJ):
        beginning(j)
    use(x)
    for step in range(1, H + 1):
        for j in range(NJ):
            if step > 1 or j > 1:
                relay(step, j)
        if step < H:
            use(xa(-step))
            use(xa(step))
            for k in range((step - 1) * X // (H - 1), step * X // (H - 1)):
                spread(k)
    use(xa(H))

    lane = lax.broadcasted_iota(jnp.int32, (1, R), 1)
    lo = lane < HR

    def doubled(v, half):
        turned = pltpu.roll(v, HR, 1)
        return jnp.where(lo, v, turned) if half == 0 else jnp.where(lo, turned, v)

    hidden = doubled(acc[pl.ds(0, CF), :], 0)
    back = doubled(acc[pl.ds(CF, CF), :], 1)
    logit = doubled(acc[pl.ds(2 * CF, 8), :], 0)[0:1]
    gating = 1.0 / (1.0 + jnp.exp(-logit))
    c0 = 0.7978845608028654
    c1 = 0.044715
    sq = hidden * hidden
    th = jnp.tanh(c0 * (hidden + c1 * (sq * hidden)))
    cdf = 0.5 * (1.0 + th)
    act = hidden * cdf
    slope = cdf + (0.5 * hidden) * (1.0 - th * th) * (c0 * (1.0 + (3.0 * c1) * sq))
    zero = jnp.zeros_like(hidden)
    pre = slope * (gating * back)
    pre_lo = jnp.where(lo, pre, zero).astype(BF)
    bd[pl.ds(0, CF), :] = pre_lo
    bd[pl.ds(CF, CF), :] = jnp.where(lo, zero, pre).astype(BF)

    def partial(d):
        xx = xa(d)
        at = pl.ds(pl.multiple_of(xx * PW, PW), PW)
        pf[xx] = dot(u2[:, at], bd[...], TN).reshape(Y, CW, R)

    ahead = sorted(range(Y), key=lambda d: -min(d, Y - d))

    def pass_on(direction, m, j):
        to = (e, tid(xa(1 if direction == 0 else -1), y, core))
        k = slot(direction, m, j)
        go(outb.at[k], inb.at[k], ch_s.at[0], ch_r.at[k], to, False)

    def came(direction, m, j):
        k = slot(direction, m, j)
        got(inb.at[k], ch_s.at[0], ch_r.at[k])
        return inb[k].astype(F32)

    partial(H)
    for j in range(Y):
        direction = 0 if j in halves[0] else 1
        outb[slot(direction, 1, j)] = pf[xa(H), ya(ahead[j])].astype(BF)
        pass_on(direction, 1, j)

    l2[pl.ds(0, CF), :] = pre_lo
    l2[pl.ds(CF, CF), :] = jnp.where(lo, zero, act * gating).astype(BF)
    gp[...] = jnp.sum(act.astype(BF).astype(F32) * back, axis=0, keepdims=True)
    for dy in range(1, Y):
        go(gp, gy.at[dy], gy_s.at[dy], gy_r.at[dy], (e, tid(x, ya(dy), core)))
    def grads(k):
        at = pl.ds(k * SW, SW)
        gr[:, at] = dot(l2[...], xg[at, :], NT).astype(BF)

    done = 0
    for m in range(2, H + 1):
        if m == 2:
            partial(H - 1)
            partial(1 - H)
        for first_part in (True, False):
            if m == 2 and not first_part:
                for d in range(H - 2, 0, -1):
                    partial(d)
                    partial(-d)
                partial(0)
            for j in range(Y):
                for direction in range(2):
                    late = j in halves[direction]
                    if late == first_part:
                        continue
                    dest = xa((H + 1 - m) * (1 if direction == 0 else -1))
                    value = pf[dest, ya(ahead[j])]
                    if m > 2 or late:
                        value = value + came(direction, m - 1, j)
                    outb[slot(direction, m, j)] = value.astype(BF)
                    pass_on(direction, m, j)
        if m == 2:
            total = gp[...]
            for dy in range(1, Y):
                got(gy.at[dy], gy_s.at[dy], gy_r.at[dy])
                total = total + gy[dy]
            gs[...] = total
            for dx in range(1, X):
                go(gs, gx.at[dx], gx_s.at[dx], gx_r.at[dx], (e, tid(xa(dx), y, core)))
        for _ in range(X // (H - 1)):
            grads(done)
            done += 1
    while done < X:
        grads(done)
        done += 1
    outs = [
        pltpu.make_async_copy(gr.at[mine], ug_hbm.at[mine], osem.at[0]),
        pltpu.make_async_copy(gr.at[mine_dn], dg_hbm.at[mine], osem.at[1]),
    ]
    for copy in outs:
        copy.start()
    go(gr.at[his], ug_hbm.at[mine], g_s.at[0], g_r.at[0], sib)
    go(gr.at[his_dn], dg_hbm.at[mine], g_s.at[1], g_r.at[1], sib)

    gate_total = gs[...]
    for dx in range(1, X):
        got(gx.at[dx], gx_s.at[dx], gx_r.at[dx])
        gate_total = gate_total + gx[dx]
    slopes = gate_total * gating * (1.0 - gating)
    srow = lax.broadcasted_iota(jnp.int32, (KP, R), 0)
    one_row = jnp.where((srow == 0) & lo, slopes, 0.0)
    hi = one_row.astype(BF)
    rest = one_row - hi.astype(F32)
    mid = rest.astype(BF)
    low = (rest - mid.astype(F32)).astype(BF)

    def embed_part(tt):
        xs = xg[pl.ds(pl.multiple_of(tt * CW, CW), CW), :]
        return (dot(hi, xs, NT) + dot(mid, xs, NT) + dot(low, xs, NT))[0:8]

    ego[...] = jnp.concatenate(
        [embed_part(tid(x, y, other)), jnp.zeros((8, 128 - CW), F32)], axis=1
    )
    go(ego, egi, e_s.at[0], e_r.at[0], sib)
    own_part = embed_part(t)[0:1]
    prow = lax.broadcasted_iota(jnp.int32, (CW, D), 0)
    pcol = lax.broadcasted_iota(jnp.int32, (CW, D), 1)
    erows = w[pl.ds(2 * CF, KP), :]
    ecol = [
        dot(ones_where(pcol == prow + (chip * CH + c * CW)), erows, NT)[:, 0:1] for c in range(2)
    ]
    outer = jnp.where(lo, ecol[0], ecol[1]) * slopes
    for el in range(2):
        otq[el] = dot(by_expert(el), ot[...], NT).astype(BF)

    for j in range(Y):
        dy = ahead[j]
        value = pf[x, ya(dy)] + came(0, H, j) + came(1, H, j)
        if dy:
            yo[dy] = value.astype(BF)
            go(yo.at[dy], yi.at[dy], yr_s.at[dy], yr_r.at[dy], (e, tid(x, ya(dy), core)))
        else:
            summed = value + outer
    n_half = (2 * H - 1) * Y
    gone(xg.at[pl.ds(0, n_half * CH)], ring_s.at[0], ring_r.at[0])
    gone(outb.at[pl.ds(0, n_half)], ch_s.at[0], ch_r.at[0])
    for dy in sorted(range(1, Y), key=lambda d: min(d, Y - d)):
        got(yi.at[dy], yr_s.at[dy], yr_r.at[dy])
        summed = summed + yi[dy].astype(F32)
    summed = summed.astype(BF)

    pad = jnp.zeros((NQ, 128 - CW), BF)
    for c in range(2):
        block = dot(bh[c], summed, NT).astype(BF)
        sbuf2[pl.ds(c * NE, NE)] = jnp.concatenate([block, pad], axis=1).reshape(NE, KP, 128)
    for rel, o in pairs:
        to = core if rel == 0 else other
        go(
            sbuf2.at[to * NE + ea(o)], rbuf2.at[core * NE + e],
            b_s.at[0], b_r.at[0], (ea(o), tid(x, y, to)), False,
        )
    rbuf2[core * NE + e] = sbuf2[core * NE + e]
    drain()
    got(egi, e_s.at[0], e_r.at[0])
    row2 = lax.broadcasted_iota(jnp.int32, (2, CW), 0)
    egv[...] = jnp.where(row2 == core, own_part, egi[...][0:1, :CW])
    outs.append(pltpu.make_async_copy(egv, eg_hbm, osem.at[2]))
    outs[-1].start()
    got(ug_hbm.at[his], g_s.at[0], g_r.at[0])
    got(dg_hbm.at[his], g_s.at[1], g_r.at[1])
    gone(sbuf2.at[pl.ds(0, 2 * NE - 1)], b_s.at[0], b_r.at[0])
    got(rbuf2.at[pl.ds(0, 2 * NE - 1)], b_s.at[0], b_r.at[0])
    placed = sum(
        dot(rbuf2[pl.ds(el * NE, NE)].reshape(NQ, 128)[:, :CW], otq[el], TN) for el in range(2)
    )
    tgv[...] = (both[pl.ds(CW, CW), :].astype(F32) + placed).astype(BF)
    outs.append(pltpu.make_async_copy(tgv, tg_hbm, osem.at[3]))
    outs[-1].start()
    for copy in outs:
        copy.wait()


def hand_over(*refs):
    ins, outs, held, sems = refs[:4], refs[4:8], refs[8:12], refs[12]
    first = [pltpu.make_async_copy(ins[i], held[i], sems.at[i]) for i in range(4)]
    second = [pltpu.make_async_copy(held[i], outs[i], sems.at[4 + i]) for i in range(4)]
    for copy in first:
        copy.start()
    for i in range(4):
        first[i].wait()
        second[i].start()
    for copy in second:
        copy.wait()


def local(groups, tensors, tokens, cotangent, routing, up_weight, down_weight, expert_embed):
    rows, cw = tokens.shape
    el, depth, fl = up_weight.shape
    sl = rows // (groups * el)
    xs = tensors // (2 * Y)
    dims = (groups, sl, cw, xs, fl)
    h = xs // 2
    cf = 2 * fl
    vm = pltpu.VMEM
    dma = pltpu.SemaphoreType.DMA
    n_ring = 2 * (h + 1) * Y

    def pair(n):
        return [dma((n,)), dma((n,))]

    scratch = [
        vm((2 * cw, rows), BF),
        vm((1, rows), jnp.int32),
        vm((el, depth), BF),
        vm((rows, rows), BF),
        vm((2, groups * KP, rows), BF),
        vm((2, groups * KP, rows), BF),
        vm((2 * groups, KP, 2 * cw + 64), BF),
        vm((2 * groups, KP, 2 * cw + 64), BF),
        vm((depth, rows), BF),
        vm((2 * cf + KP, depth), BF),
        vm((2 * cf, depth // 2), BF),
        vm((2 * cf + KP, rows), F32),
        vm((2 * cf, rows), BF),
        vm((2 * cf, rows), BF),
        vm((2 * cf, depth), BF),
        vm((xs, Y, cw, rows), F32),
        vm((2 * (h + 1) * Y, cw, rows), BF),
        vm((2 * (h + 1) * Y, cw, rows), BF),
        vm((Y, cw, rows), BF),
        vm((Y, cw, rows), BF),
        vm((1, rows), F32),
        vm((Y, 1, rows), F32),
        vm((1, rows), F32),
        vm((xs, 1, rows), F32),
        vm((8, 128), F32),
        vm((8, 128), F32),
        vm((el, cw), F32),
        vm((cw, rows), BF),
        vm((2 * groups, KP, 128), BF),
        vm((2 * groups, KP, 128), BF),
        dma((6,)),
        dma((4,)),
        *pair(2),
        *pair(1),
        *pair(2 * Y),
        dma((1,)), dma((2 * n_ring,)),
        dma((1,)), dma((n_ring,)),
        *pair(Y),
        *pair(Y),
        *pair(xs),
        *pair(2),
        *pair(1),
        *pair(1),
    ]
    hbm = pl.BlockSpec(memory_space=pl.ANY)
    shapes = (
        jax.ShapeDtypeStruct((cw, rows), BF),
        jax.ShapeDtypeStruct((el * fl, depth), BF),
        jax.ShapeDtypeStruct((el * fl, depth), BF),
        jax.ShapeDtypeStruct((el, cw), F32),
    )
    made = pl.pallas_call(
        functools.partial(kernel, dims),
        out_shape=shapes,
        in_specs=[hbm] * 6,
        out_specs=(hbm,) * 4,
        scratch_shapes=scratch,
        compiler_params=pltpu.CompilerParams(
            collective_id=0, has_side_effects=True, vmem_limit_bytes=60 * 1024 * 1024
        ),
    )(
        tokens.T,
        cotangent.T,
        routing,
        up_weight.transpose(0, 2, 1).reshape(el * fl, depth),
        down_weight.reshape(el * fl, depth),
        expert_embed,
    )
    tg, ug, dg, eg = pl.pallas_call(
        hand_over,
        out_shape=shapes,
        in_specs=[hbm] * 4,
        out_specs=(hbm,) * 4,
        scratch_shapes=[vm(shape.shape, shape.dtype) for shape in shapes] + [dma((8,))],
        compiler_params=pltpu.CompilerParams(vmem_limit_bytes=60 * 1024 * 1024),
    )(*made)
    return (
        tg.T,
        ug.reshape(el, fl, depth).transpose(0, 2, 1),
        dg.reshape(el, fl, depth),
        eg,
    )


def solution(mesh):
    return jax.shard_map(
        functools.partial(local, mesh.shape["expert"], mesh.shape["tensor"]),
        mesh=mesh,
        in_specs=(
            P("expert", "tensor"),
            P("expert", "tensor"),
            P("expert", None),
            P("expert", None, "tensor"),
            P("expert", "tensor", None),
            P("expert", None),
        ),
        out_specs=(
            P("expert", "tensor"),
            P("expert", None, "tensor"),
            P("expert", "tensor", None),
            P("expert", "tensor"),
        ),
        check_vma=False,
    )
```

```python
import functools

import jax
import jax.numpy as jnp
from jax import lax
from jax.experimental import pallas as pl
from jax.experimental.pallas import tpu as pltpu
from jax.sharding import PartitionSpec as P

Y = 4
KP = 16
CUT = 32
BF = jnp.bfloat16
F32 = jnp.float32
NN = ((1,), (0,))
NT = ((1,), (1,))
TN = ((0,), (0,))


def dot(a, b, dims):
    return lax.dot_general(a, b, (dims, ((), ())), preferred_element_type=F32)


def remote(src, dst, ssem, rsem, device):
    return pltpu.make_async_remote_copy(
        src_ref=src,
        dst_ref=dst,
        send_sem=ssem,
        recv_sem=rsem,
        device_id=device,
        device_id_type=pl.DeviceIdType.MESH,
    )


def ones_where(hit):
    return hit.astype(F32).astype(BF)


def kernel(
    dims,
    tok_hbm, cot_hbm, rt_hbm, up_hbm, down_hbm, emb_hbm,
    tg_hbm, ug_hbm, dg_hbm, eg_hbm,
    both, rt, emb, ot, otq, bh, ec, sbuf, rbuf, xg, w, u2, acc, l2, bd, gr,
    pf, outb, inb, yo, yi, gp, gy, gs, gx, ego, egi, egv, tgv, sbuf2, rbuf2,
    lsem, osem,
    w_s, w_r, a_s, a_r, y_s, y_r, ring_s, ring_r, ch_s, ch_r, yr_s, yr_r,
    gy_s, gy_r, gx_s, gx_r, g_s, g_r, e_s, e_r, b_s, b_r,
):
    NE, SL, CW, X, FL = dims
    H = X // 2
    HR = NE * SL
    R = 2 * HR
    NQ = NE * KP
    CF = 2 * FL
    SW = Y * 2 * CW
    CH = 2 * CW
    PW = Y * CW
    D = X * SW
    e = lax.axis_index("expert")
    t = lax.axis_index("tensor")
    core = lax.rem(t, 2)
    chip = t // 2
    y = lax.rem(chip, Y)
    x = chip // Y
    other = 1 - core

    def xa(d):
        return lax.rem(x + (d + X), X)

    def ya(d):
        return lax.rem(y + (d + Y), Y)

    def ea(d):
        return lax.rem(e + (d + NE), NE)

    def tid(xx, yy, cc):
        return (xx * Y + yy) * 2 + cc

    sib = (e, tid(x, y, other))
    sends = []

    def go(src, dst, ssem, rsem, device, single=True):
        copy = remote(src, dst, ssem, rsem, device)
        copy.start()
        if single:
            sends.append(copy)

    def gone(src, ssem, rsem):
        remote(src, src, ssem, rsem, sib).wait_send()

    def drain():
        for copy in sends:
            copy.wait_send()
        sends.clear()

    def got(dst, ssem, rsem):
        remote(dst, dst, ssem, rsem, sib).wait_recv()

    barrier = pltpu.get_barrier_semaphore()
    pairs = [(rel, o) for o in range(NE) for rel in range(2) if rel or o]
    pairs.sort(key=lambda p: -min(p[1], NE - p[1]))
    peers = [(ea(o), tid(x, y, core if rel == 0 else other)) for rel, o in pairs]
    peers += [(e, tid(x, ya(dy), core)) for dy in range(1, Y)]
    peers += [(e, tid(xa(dx), y, core)) for dx in range(1, X)]
    loads = [
        pltpu.make_async_copy(rt_hbm, rt, lsem.at[0]),
        pltpu.make_async_copy(tok_hbm, both.at[pl.ds(0, CW)], lsem.at[1]),
        pltpu.make_async_copy(cot_hbm, both.at[pl.ds(CW, CW)], lsem.at[2]),
        pltpu.make_async_copy(emb_hbm, emb, lsem.at[3]),
        pltpu.make_async_copy(
            up_hbm.at[pl.ds(pl.multiple_of(core * FL, FL), FL)],
            w.at[pl.ds(pl.multiple_of(core * FL, FL), FL)],
            lsem.at[4],
        ),
        pltpu.make_async_copy(
            down_hbm.at[pl.ds(pl.multiple_of(core * FL, FL), FL)],
            w.at[pl.ds(pl.multiple_of(CF + core * FL, FL), FL)],
            lsem.at[5],
        ),
    ]
    for copy in loads[:3]:
        copy.start()
    for peer in peers:
        pl.semaphore_signal(barrier, inc=1, device_id=peer, device_id_type=pl.DeviceIdType.MESH)
    for copy in loads[3:]:
        copy.start()

    qrow = lax.broadcasted_iota(jnp.int32, (NQ, R), 0)
    qcol = lax.broadcasted_iota(jnp.int32, (NQ, R), 1)
    qg = lax.shift_right_logical(qrow, 4)
    qk = lax.bitwise_and(qrow, KP - 1)

    def by_expert(el):
        return ones_where((qcol == qg * (2 * SL) + el * SL + qk) & (qk < SL))

    def by_half(half):
        return ones_where((qcol == half * HR + qg * SL + qk) & (qk < SL))

    for copy in loads[:3]:
        copy.wait()
    tok_of = lax.broadcasted_iota(jnp.int32, (R, R), 0)
    ot[...] = ones_where(tok_of == rt[...])
    ordered = dot(both[...], ot[...], NN).astype(BF)
    pad = jnp.zeros((NQ, 64), BF)
    for el in range(2):
        block = dot(by_expert(el), ordered, NT).astype(BF)
        sbuf[pl.ds(el * NE, NE)] = jnp.concatenate([block, pad], axis=1).reshape(NE, KP, CH + 64)
    pl.semaphore_wait(barrier, len(peers))

    for rel, o in pairs:
        to = core if rel == 0 else other
        go(
            sbuf.at[to * NE + ea(o)], rbuf.at[core * NE + e],
            a_s.at[0], a_r.at[0], (ea(o), tid(x, y, to)), False,
        )
    rbuf[core * NE + e] = sbuf[core * NE + e]
    mine = pl.ds(pl.multiple_of(core * FL, FL), FL)
    mine_dn = pl.ds(pl.multiple_of(CF + core * FL, FL), FL)
    his = pl.ds(pl.multiple_of(other * FL, FL), FL)
    his_dn = pl.ds(pl.multiple_of(CF + other * FL, FL), FL)
    go(up_hbm.at[his], w.at[mine], w_s.at[0], w_r.at[0], sib)
    go(down_hbm.at[his], w.at[mine_dn], w_s.at[1], w_r.at[1], sib)
    acc[...] = jnp.zeros_like(acc)
    for c in range(2):
        bh[c] = by_half(c)
        otq[c] = dot(by_expert(c), ot[...], NT).astype(BF)
    got(rbuf.at[pl.ds(0, 2 * NE - 1)], a_s.at[0], a_r.at[0])
    for c in range(2):
        landed = rbuf[pl.ds(c * NE, NE)].reshape(NQ, CH + 64)
        part = dot(landed[:, :CW], bh[0], TN) + dot(landed[:, CW:CH], bh[1], TN)
        xg[pl.ds(pl.multiple_of(chip * CH + c * CW, CW), CW), :] = part.astype(BF)

    def chunk(xx, yy, half):
        return xg.at[pl.ds(pl.multiple_of((xx * Y + yy) * CH + half * CW, CW), CW)]

    near = sorted(range(1, Y), key=lambda d: min(d, Y - d))
    beside = [dy for dy in near if min(dy, Y - dy) == 1]
    beyond = [dy for dy in near if min(dy, Y - dy) > 1]
    order = [(0, 0), (0, 1)]
    order += [(dy, half) for group in (beside, beyond) for half in range(2) for dy in group]
    NJ = len(order)

    def gslot(direction, step, j):
        return (direction * (H + 1) + step) * NJ + j

    halves = (set(range(Y // 2)), set(range(Y // 2, Y)))

    def slot(direction, step, j):
        return (direction * (H + 1) + step) * Y + j

    def onward(direction, step, j, piece):
        to = (e, tid(xa(1 if direction == 0 else -1), y, core))
        k = gslot(direction, step, j)
        go(piece, piece, ring_s.at[0], ring_r.at[k], to, False)

    for j in range(2):
        for direction in range(2):
            onward(direction, 1, j, chunk(x, y, j))
    for dy, half in order[2:]:
        own = chunk(x, y, half)
        k = dy * 2 + half
        go(own, own, y_s.at[k], y_r.at[k], (e, tid(x, ya(dy), core)))

    drain()
    gone(sbuf.at[pl.ds(0, 2 * NE - 1)], a_s.at[0], a_r.at[0])
    for copy in loads[3:]:
        copy.wait()
    got(w.at[his], w_s.at[0], w_r.at[0])
    got(w.at[his_dn], w_s.at[1], w_r.at[1])
    erow = lax.broadcasted_iota(jnp.int32, (KP, D), 0)
    both_emb = emb[...].astype(F32)
    own_emb = jnp.where(core == 0, both_emb[0:1], both_emb[1:2])
    w[pl.ds(2 * CF, KP), :] = jnp.where(erow == 0, own_emb, 0.0).astype(BF)

    prow = lax.broadcasted_iota(jnp.int32, (CW, D), 0)
    pcol = lax.broadcasted_iota(jnp.int32, (CW, D), 1)
    erows = w[pl.ds(2 * CF, KP), :]
    ecol = [
        dot(ones_where(pcol == prow + (chip * CH + c * CW)), erows, NT)[:, 0:1] for c in range(2)
    ]
    lane = lax.broadcasted_iota(jnp.int32, (1, R), 1)
    lo = lane < HR
    ec[...] = jnp.where(lo, ecol[0], ecol[1])

    def spread(xx):
        at = pl.ds(xx * SW, SW)
        srow = lax.broadcasted_iota(jnp.int32, (SW, PW), 0)
        scol = lax.broadcasted_iota(jnp.int32, (SW, PW), 1)
        src = (scol // CW) * CH + lax.rem(scol, CW)
        for c in range(2):
            pick = ones_where(srow == src + c * CW)
            u2[pl.ds(c * CF, CF), pl.ds(xx * PW, PW)] = dot(w[pl.ds(0, CF), at], pick, NN).astype(BF)

    def use(xx):
        at = pl.ds(pl.multiple_of(xx * SW, SW), SW)
        acc[...] += dot(w[:, at], xg[at, :], NN)

    def relay(step, j):
        dy, half = order[j]
        for direction in range(2):
            if step == H and half != direction:
                continue
            piece = chunk(xa(-step if direction == 0 else step), ya(-dy), half)
            got(piece, ring_s.at[0], ring_r.at[gslot(direction, step, j)])
            if step < H - 1 or (step == H - 1 and half == direction):
                onward(direction, step + 1, j, piece)

    def beginning(j):
        dy, half = order[j]
        piece = chunk(x, ya(-dy), half)
        k = dy * 2 + half
        got(piece, y_s.at[k], y_r.at[k])
        onward(0, 1, j, piece)
        onward(1, 1, j, piece)

    lead = 2 + len(beside)
    for j in range(2, lead):
        beginning(j)
    relay(1, 0)
    relay(1, 1)
    for j in range(lead, NJ):
        beginning(j)
    use(x)
    for step in range(1, H + 1):
        for j in range(NJ):
            if step > 1 or j > 1:
                relay(step, j)
        if step < H:
            use(xa(-step))
            use(xa(step))
            for k in range((step - 1) * X // (H - 1), step * X // (H - 1)):
                spread(k)
    use(xa(H))


    def doubled(v, half):
        turned = pltpu.roll(v, HR, 1)
        return jnp.where(lo, v, turned) if half == 0 else jnp.where(lo, turned, v)

    hidden = doubled(acc[pl.ds(0, CF), :], 0)
    back = doubled(acc[pl.ds(CF, CF), :], 1)
    logit = doubled(acc[pl.ds(2 * CF, 8), :], 0)[0:1]
    gating = 1.0 / (1.0 + jnp.exp(-logit))
    c0 = 0.7978845608028654
    c1 = 0.044715
    sq = hidden * hidden
    th = jnp.tanh(c0 * (hidden + c1 * (sq * hidden)))
    cdf = 0.5 * (1.0 + th)
    act = hidden * cdf
    slope = cdf + (0.5 * hidden) * (1.0 - th * th) * (c0 * (1.0 + (3.0 * c1) * sq))
    zero = jnp.zeros_like(hidden)
    pre = slope * (gating * back)
    pre_lo = jnp.where(lo, pre, zero).astype(BF)
    bd[pl.ds(0, CF), :] = pre_lo
    bd[pl.ds(CF, CF), :] = jnp.where(lo, zero, pre).astype(BF)

    def partial(d):
        xx = xa(d)
        at = pl.ds(pl.multiple_of(xx * PW, PW), PW)
        pf[xx] = dot(u2[:, at], bd[...], TN).reshape(Y, CW, R)

    ahead = sorted(range(Y), key=lambda d: -min(d, Y - d))

    def pass_on(direction, m, j, hops=1):
        to = (e, tid(xa(hops if direction == 0 else -hops), y, core))
        k = slot(direction, m, j)
        go(outb.at[k], inb.at[k], ch_s.at[0], ch_r.at[k], to, False)

    def came(direction, m, j):
        k = slot(direction, m, j)
        got(inb.at[k], ch_s.at[0], ch_r.at[k])
        return inb[k].astype(F32)

    partial(H)
    for j in range(Y):
        direction = 0 if j in halves[0] else 1
        outb[slot(direction, 1, j)] = pf[xa(H), ya(ahead[j])].astype(BF)
        pass_on(direction, 1, j, 2)

    l2[pl.ds(0, CF), :] = pre_lo
    l2[pl.ds(CF, CF), :] = jnp.where(lo, zero, act * gating).astype(BF)
    gp[...] = jnp.sum(act.astype(BF).astype(F32) * back, axis=0, keepdims=True)
    for dy in range(1, Y):
        go(gp, gy.at[dy], gy_s.at[dy], gy_r.at[dy], (e, tid(x, ya(dy), core)))
    def grads(k):
        at = pl.ds(k * SW, SW)
        gr[:, at] = dot(l2[...], xg[at, :], NT).astype(BF)

    done = 0
    for m in range(2, H + 1):
        if m == 2:
            partial(H - 1)
            partial(1 - H)
        if m == 3:
            for d in range(H - 2, 0, -1):
                partial(d)
                partial(-d)
            partial(0)
        for late in (True, False):
            for j in range(Y):
                for direction in range(2):
                    if (j in halves[direction]) != late:
                        continue
                    dest = xa((H + 1 - m) * (1 if direction == 0 else -1))
                    value = pf[dest, ya(ahead[j])]
                    if m == 3 and late:
                        value = value + came(direction, 1, j)
                    if m > 2:
                        value = value + came(direction, m - 1, j)
                    outb[slot(direction, m, j)] = value.astype(BF)
                    pass_on(direction, m, j)
        if m == 2:
            total = gp[...]
            for dy in range(1, Y):
                got(gy.at[dy], gy_s.at[dy], gy_r.at[dy])
                total = total + gy[dy]
            gs[...] = total
            for dx in range(1, X):
                go(gs, gx.at[dx], gx_s.at[dx], gx_r.at[dx], (e, tid(xa(dx), y, core)))
        for _ in range(X // (H - 1)):
            grads(done)
            done += 1
    while done < X:
        grads(done)
        done += 1
    outs = [
        pltpu.make_async_copy(gr.at[mine], ug_hbm.at[mine], osem.at[0]),
        pltpu.make_async_copy(gr.at[mine_dn], dg_hbm.at[mine], osem.at[1]),
    ]
    for copy in outs:
        copy.start()
    go(gr.at[his], ug_hbm.at[mine], g_s.at[0], g_r.at[0], sib)
    go(gr.at[his_dn], dg_hbm.at[mine], g_s.at[1], g_r.at[1], sib)

    gate_total = gs[...]
    for dx in range(1, X):
        got(gx.at[dx], gx_s.at[dx], gx_r.at[dx])
        gate_total = gate_total + gx[dx]
    slopes = gate_total * gating * (1.0 - gating)
    srow = lax.broadcasted_iota(jnp.int32, (KP, R), 0)
    one_row = jnp.where((srow == 0) & lo, slopes, 0.0)
    hi = one_row.astype(BF)
    rest = one_row - hi.astype(F32)
    mid = rest.astype(BF)
    low = (rest - mid.astype(F32)).astype(BF)

    def embed_part(tt):
        xs = xg[pl.ds(pl.multiple_of(tt * CW, CW), CW), :]
        return (dot(hi, xs, NT) + dot(mid, xs, NT) + dot(low, xs, NT))[0:8]

    ego[...] = jnp.concatenate(
        [embed_part(tid(x, y, other)), jnp.zeros((8, 128 - CW), F32)], axis=1
    )
    go(ego, egi, e_s.at[0], e_r.at[0], sib)
    own_part = embed_part(t)[0:1]
    outer = ec[...] * slopes
    for j in range(Y):
        dy = ahead[j]
        value = pf[x, ya(dy)] + came(0, H, j) + came(1, H, j)
        if dy:
            yo[dy] = value.astype(BF)
            go(yo.at[dy], yi.at[dy], yr_s.at[dy], yr_r.at[dy], (e, tid(x, ya(dy), core)))
        else:
            summed = value + outer
    n_half = (2 * H - 1) * Y
    gone(xg.at[pl.ds(0, n_half * CH)], ring_s.at[0], ring_r.at[0])
    gone(outb.at[pl.ds(0, n_half)], ch_s.at[0], ch_r.at[0])
    for dy in sorted(range(1, Y), key=lambda d: min(d, Y - d)):
        got(yi.at[dy], yr_s.at[dy], yr_r.at[dy])
        summed = summed + yi[dy].astype(F32)
    summed = summed.astype(BF)

    pad = jnp.zeros((NQ, 128 - CW), BF)
    for c in range(2):
        block = dot(bh[c], summed, NT).astype(BF)
        sbuf2[pl.ds(c * NE, NE)] = jnp.concatenate([block, pad], axis=1).reshape(NE, KP, 128)
    for rel, o in pairs:
        to = core if rel == 0 else other
        go(
            sbuf2.at[to * NE + ea(o)], rbuf2.at[core * NE + e],
            b_s.at[0], b_r.at[0], (ea(o), tid(x, y, to)), False,
        )
    rbuf2[core * NE + e] = sbuf2[core * NE + e]
    drain()
    got(egi, e_s.at[0], e_r.at[0])
    row2 = lax.broadcasted_iota(jnp.int32, (2, CW), 0)
    egv[...] = jnp.where(row2 == core, own_part, egi[...][0:1, :CW])
    outs.append(pltpu.make_async_copy(egv, eg_hbm, osem.at[2]))
    outs[-1].start()
    got(ug_hbm.at[his], g_s.at[0], g_r.at[0])
    got(dg_hbm.at[his], g_s.at[1], g_r.at[1])
    gone(sbuf2.at[pl.ds(0, 2 * NE - 1)], b_s.at[0], b_r.at[0])
    got(rbuf2.at[pl.ds(0, 2 * NE - 1)], b_s.at[0], b_r.at[0])
    placed = sum(
        dot(rbuf2[pl.ds(el * NE, NE)].reshape(NQ, 128)[:, :CW], otq[el], TN) for el in range(2)
    )
    tgv[...] = (both[pl.ds(CW, CW), :].astype(F32) + placed).astype(BF)
    outs.append(pltpu.make_async_copy(tgv, tg_hbm, osem.at[3]))
    outs[-1].start()
    for copy in outs:
        copy.wait()


def hand_over(*refs):
    ins, outs, held, sems = refs[:4], refs[4:8], refs[8:12], refs[12]
    places = [(i, pl.ds(r, CUT)) for r in range(0, ins[1].shape[0], CUT) for i in (1, 2)]
    places += [(0, pl.ds(0, ins[0].shape[0])), (3, pl.ds(0, ins[3].shape[0]))]
    n = len(places)
    first, second = [], []
    for k, (i, at) in enumerate(places):
        first.append(pltpu.make_async_copy(ins[i].at[at], held[i].at[at], sems.at[k]))
        second.append(pltpu.make_async_copy(held[i].at[at], outs[i].at[at], sems.at[n + k]))
        first[k].start()
    for k in range(n):
        first[k].wait()
        second[k].start()
    for copy in second:
        copy.wait()


def local(groups, tensors, tokens, cotangent, routing, up_weight, down_weight, expert_embed):
    rows, cw = tokens.shape
    el, depth, fl = up_weight.shape
    sl = rows // (groups * el)
    xs = tensors // (2 * Y)
    dims = (groups, sl, cw, xs, fl)
    h = xs // 2
    cf = 2 * fl
    vm = pltpu.VMEM
    dma = pltpu.SemaphoreType.DMA
    n_ring = 2 * (h + 1) * Y

    def pair(n):
        return [dma((n,)), dma((n,))]

    scratch = [
        vm((2 * cw, rows), BF),
        vm((1, rows), jnp.int32),
        vm((el, depth), BF),
        vm((rows, rows), BF),
        vm((2, groups * KP, rows), BF),
        vm((2, groups * KP, rows), BF),
        vm((cw, rows), F32),
        vm((2 * groups, KP, 2 * cw + 64), BF),
        vm((2 * groups, KP, 2 * cw + 64), BF),
        vm((depth, rows), BF),
        vm((2 * cf + KP, depth), BF),
        vm((2 * cf, depth // 2), BF),
        vm((2 * cf + KP, rows), F32),
        vm((2 * cf, rows), BF),
        vm((2 * cf, rows), BF),
        vm((2 * cf, depth), BF),
        vm((xs, Y, cw, rows), F32),
        vm((2 * (h + 1) * Y, cw, rows), BF),
        vm((2 * (h + 1) * Y, cw, rows), BF),
        vm((Y, cw, rows), BF),
        vm((Y, cw, rows), BF),
        vm((1, rows), F32),
        vm((Y, 1, rows), F32),
        vm((1, rows), F32),
        vm((xs, 1, rows), F32),
        vm((8, 128), F32),
        vm((8, 128), F32),
        vm((el, cw), F32),
        vm((cw, rows), BF),
        vm((2 * groups, KP, 128), BF),
        vm((2 * groups, KP, 128), BF),
        dma((6,)),
        dma((4,)),
        *pair(2),
        *pair(1),
        *pair(2 * Y),
        dma((1,)), dma((2 * n_ring,)),
        dma((1,)), dma((n_ring,)),
        *pair(Y),
        *pair(Y),
        *pair(xs),
        *pair(2),
        *pair(1),
        *pair(1),
    ]
    hbm = pl.BlockSpec(memory_space=pl.ANY)
    shapes = (
        jax.ShapeDtypeStruct((cw, rows), BF),
        jax.ShapeDtypeStruct((el * fl, depth), BF),
        jax.ShapeDtypeStruct((el * fl, depth), BF),
        jax.ShapeDtypeStruct((el, cw), F32),
    )
    made = pl.pallas_call(
        functools.partial(kernel, dims),
        out_shape=shapes,
        in_specs=[hbm] * 6,
        out_specs=(hbm,) * 4,
        scratch_shapes=scratch,
        compiler_params=pltpu.CompilerParams(
            collective_id=0, has_side_effects=True, vmem_limit_bytes=60 * 1024 * 1024
        ),
    )(
        tokens.T,
        cotangent.T,
        routing,
        up_weight.transpose(0, 2, 1).reshape(el * fl, depth),
        down_weight.reshape(el * fl, depth),
        expert_embed,
    )
    tg, ug, dg, eg = pl.pallas_call(
        hand_over,
        out_shape=shapes,
        in_specs=[hbm] * 4,
        out_specs=(hbm,) * 4,
        scratch_shapes=[vm(shape.shape, shape.dtype) for shape in shapes] + [dma((4 * (el * fl // CUT) + 4,))],
        compiler_params=pltpu.CompilerParams(vmem_limit_bytes=60 * 1024 * 1024),
    )(*made)
    return (
        tg.T,
        ug.reshape(el, fl, depth).transpose(0, 2, 1),
        dg.reshape(el, fl, depth),
        eg,
    )


def solution(mesh):
    return jax.shard_map(
        functools.partial(local, mesh.shape["expert"], mesh.shape["tensor"]),
        mesh=mesh,
        in_specs=(
            P("expert", "tensor"),
            P("expert", "tensor"),
            P("expert", None),
            P("expert", None, "tensor"),
            P("expert", "tensor", None),
            P("expert", None),
        ),
        out_specs=(
            P("expert", "tensor"),
            P("expert", None, "tensor"),
            P("expert", "tensor", None),
            P("expert", "tensor"),
        ),
        check_vma=False,
    )
```

```python
import functools

import jax
import jax.numpy as jnp
from jax import lax
from jax.experimental import pallas as pl
from jax.experimental.pallas import tpu as pltpu
from jax.sharding import PartitionSpec as P

Y = 4
KP = 16
CUT = 32
BF = jnp.bfloat16
F32 = jnp.float32
NN = ((1,), (0,))
NT = ((1,), (1,))
TN = ((0,), (0,))


def dot(a, b, dims):
    return lax.dot_general(a, b, (dims, ((), ())), preferred_element_type=F32)


def remote(src, dst, ssem, rsem, device):
    return pltpu.make_async_remote_copy(
        src_ref=src,
        dst_ref=dst,
        send_sem=ssem,
        recv_sem=rsem,
        device_id=device,
        device_id_type=pl.DeviceIdType.MESH,
    )


def ones_where(hit):
    return hit.astype(F32).astype(BF)


def kernel(
    dims,
    tok_hbm, cot_hbm, rt_hbm, up_hbm, down_hbm, emb_hbm,
    tg_hbm, ug_hbm, dg_hbm, eg_hbm,
    both, rt, emb, ot, otq, bh, ec, sbuf, rbuf, xg, w, u2, acc, l2, bd, gr,
    pf, outb, inb, yo, yi, gp, gy, gs, gx, ego, egi, egv, tgv, sbuf2, rbuf2,
    lsem, osem,
    w_s, w_r, a_s, a_r, y_s, y_r, ring_s, ring_r, ch_s, ch_r, yr_s, yr_r,
    gy_s, gy_r, gx_s, gx_r, g_s, g_r, e_s, e_r, b_s, b_r,
):
    NE, SL, CW, X, FL = dims
    H = X // 2
    HR = NE * SL
    R = 2 * HR
    NQ = NE * KP
    CF = 2 * FL
    SW = Y * 2 * CW
    CH = 2 * CW
    PW = Y * CW
    D = X * SW
    e = lax.axis_index("expert")
    t = lax.axis_index("tensor")
    core = lax.rem(t, 2)
    chip = t // 2
    y = lax.rem(chip, Y)
    x = chip // Y
    other = 1 - core

    def xa(d):
        return lax.rem(x + (d + X), X)

    def ya(d):
        return lax.rem(y + (d + Y), Y)

    def ea(d):
        return lax.rem(e + (d + NE), NE)

    def tid(xx, yy, cc):
        return (xx * Y + yy) * 2 + cc

    sib = (e, tid(x, y, other))
    sends = []

    def go(src, dst, ssem, rsem, device, single=True):
        copy = remote(src, dst, ssem, rsem, device)
        copy.start()
        if single:
            sends.append(copy)

    def gone(src, ssem, rsem):
        remote(src, src, ssem, rsem, sib).wait_send()

    def drain():
        for copy in sends:
            copy.wait_send()
        sends.clear()

    def got(dst, ssem, rsem):
        remote(dst, dst, ssem, rsem, sib).wait_recv()

    barrier = pltpu.get_barrier_semaphore()
    pairs = [(rel, o) for o in range(NE) for rel in range(2) if rel or o]
    pairs.sort(key=lambda p: -min(p[1], NE - p[1]))
    peers = [(ea(o), tid(x, y, core if rel == 0 else other)) for rel, o in pairs]
    peers += [(e, tid(x, ya(dy), core)) for dy in range(1, Y)]
    peers += [(e, tid(xa(dx), y, core)) for dx in range(1, X)]
    loads = [
        pltpu.make_async_copy(rt_hbm, rt, lsem.at[0]),
        pltpu.make_async_copy(tok_hbm, both.at[pl.ds(0, CW)], lsem.at[1]),
        pltpu.make_async_copy(cot_hbm, both.at[pl.ds(CW, CW)], lsem.at[2]),
        pltpu.make_async_copy(emb_hbm, emb, lsem.at[3]),
        pltpu.make_async_copy(
            up_hbm.at[pl.ds(pl.multiple_of(core * FL, FL), FL)],
            w.at[pl.ds(pl.multiple_of(core * FL, FL), FL)],
            lsem.at[4],
        ),
        pltpu.make_async_copy(
            down_hbm.at[pl.ds(pl.multiple_of(core * FL, FL), FL)],
            w.at[pl.ds(pl.multiple_of(CF + core * FL, FL), FL)],
            lsem.at[5],
        ),
    ]
    for copy in loads[:3]:
        copy.start()
    for peer in peers:
        pl.semaphore_signal(barrier, inc=1, device_id=peer, device_id_type=pl.DeviceIdType.MESH)
    for copy in loads[3:]:
        copy.start()

    qrow = lax.broadcasted_iota(jnp.int32, (NQ, R), 0)
    qcol = lax.broadcasted_iota(jnp.int32, (NQ, R), 1)
    qg = lax.shift_right_logical(qrow, 4)
    qk = lax.bitwise_and(qrow, KP - 1)

    def by_expert(el):
        return ones_where((qcol == qg * (2 * SL) + el * SL + qk) & (qk < SL))

    def by_half(half):
        return ones_where((qcol == half * HR + qg * SL + qk) & (qk < SL))

    for copy in loads[:3]:
        copy.wait()
    tok_of = lax.broadcasted_iota(jnp.int32, (R, R), 0)
    ot[...] = ones_where(tok_of == rt[...])
    ordered = dot(both[...], ot[...], NN).astype(BF)
    pad = jnp.zeros((NQ, 64), BF)
    for el in range(2):
        block = dot(by_expert(el), ordered, NT).astype(BF)
        sbuf[pl.ds(el * NE, NE)] = jnp.concatenate([block, pad], axis=1).reshape(NE, KP, CH + 64)
    pl.semaphore_wait(barrier, len(peers))

    for rel, o in pairs:
        to = core if rel == 0 else other
        go(
            sbuf.at[to * NE + ea(o)], rbuf.at[core * NE + e],
            a_s.at[0], a_r.at[0], (ea(o), tid(x, y, to)), False,
        )
    rbuf[core * NE + e] = sbuf[core * NE + e]
    mine = pl.ds(pl.multiple_of(core * FL, FL), FL)
    mine_dn = pl.ds(pl.multiple_of(CF + core * FL, FL), FL)
    his = pl.ds(pl.multiple_of(other * FL, FL), FL)
    his_dn = pl.ds(pl.multiple_of(CF + other * FL, FL), FL)
    go(up_hbm.at[his], w.at[mine], w_s.at[0], w_r.at[0], sib)
    go(down_hbm.at[his], w.at[mine_dn], w_s.at[1], w_r.at[1], sib)
    acc[...] = jnp.zeros_like(acc)
    for c in range(2):
        bh[c] = by_half(c)
        otq[c] = dot(by_expert(c), ot[...], NT).astype(BF)
    got(rbuf.at[pl.ds(0, 2 * NE - 1)], a_s.at[0], a_r.at[0])
    def chunk(xx, yy, half):
        return xg.at[pl.ds(pl.multiple_of((xx * Y + yy) * CH + half * CW, CW), CW)]

    near = sorted(range(1, Y), key=lambda d: min(d, Y - d))
    beside = [dy for dy in near if min(dy, Y - dy) == 1]
    beyond = [dy for dy in near if min(dy, Y - dy) > 1]
    order = [(0, 0), (0, 1)]
    order += [(dy, half) for group in (beside, beyond) for half in range(2) for dy in group]
    NJ = len(order)

    def gslot(direction, step, j):
        return (direction * (H + 1) + step) * NJ + j

    halves = (set(range(Y // 2)), set(range(Y // 2, Y)))

    def slot(direction, step, j):
        return (direction * (H + 1) + step) * Y + j

    def onward(direction, step, j, piece):
        to = (e, tid(xa(1 if direction == 0 else -1), y, core))
        k = gslot(direction, step, j)
        go(piece, piece, ring_s.at[0], ring_r.at[k], to, False)

    def make_half(c):
        landed = rbuf[pl.ds(c * NE, NE)].reshape(NQ, CH + 64)
        part = dot(landed[:, :CW], bh[0], TN) + dot(landed[:, CW:CH], bh[1], TN)
        xg[pl.ds(pl.multiple_of(chip * CH + c * CW, CW), CW), :] = part.astype(BF)

    def to_column(dy, half):
        own = chunk(x, y, half)
        k = dy * 2 + half
        go(own, own, y_s.at[k], y_r.at[k], (e, tid(x, ya(dy), core)))

    for half in range(2):
        make_half(half)
        for direction in range(2):
            onward(direction, 1, half, chunk(x, y, half))
        for dy in beside:
            to_column(dy, half)
    for half in range(2):
        for dy in beyond:
            to_column(dy, half)

    drain()
    gone(sbuf.at[pl.ds(0, 2 * NE - 1)], a_s.at[0], a_r.at[0])
    for copy in loads[3:]:
        copy.wait()
    got(w.at[his], w_s.at[0], w_r.at[0])
    got(w.at[his_dn], w_s.at[1], w_r.at[1])
    erow = lax.broadcasted_iota(jnp.int32, (KP, D), 0)
    both_emb = emb[...].astype(F32)
    own_emb = jnp.where(core == 0, both_emb[0:1], both_emb[1:2])
    w[pl.ds(2 * CF, KP), :] = jnp.where(erow == 0, own_emb, 0.0).astype(BF)

    prow = lax.broadcasted_iota(jnp.int32, (CW, D), 0)
    pcol = lax.broadcasted_iota(jnp.int32, (CW, D), 1)
    erows = w[pl.ds(2 * CF, KP), :]
    ecol = [
        dot(ones_where(pcol == prow + (chip * CH + c * CW)), erows, NT)[:, 0:1] for c in range(2)
    ]
    lane = lax.broadcasted_iota(jnp.int32, (1, R), 1)
    lo = lane < HR
    ec[...] = jnp.where(lo, ecol[0], ecol[1])

    def spread(xx):
        at = pl.ds(xx * SW, SW)
        srow = lax.broadcasted_iota(jnp.int32, (SW, PW), 0)
        scol = lax.broadcasted_iota(jnp.int32, (SW, PW), 1)
        src = (scol // CW) * CH + lax.rem(scol, CW)
        for c in range(2):
            pick = ones_where(srow == src + c * CW)
            u2[pl.ds(c * CF, CF), pl.ds(xx * PW, PW)] = dot(w[pl.ds(0, CF), at], pick, NN).astype(BF)

    def use(xx):
        at = pl.ds(pl.multiple_of(xx * SW, SW), SW)
        acc[...] += dot(w[:, at], xg[at, :], NN)

    def relay(step, j):
        dy, half = order[j]
        for direction in range(2):
            if step == H and half != direction:
                continue
            piece = chunk(xa(-step if direction == 0 else step), ya(-dy), half)
            got(piece, ring_s.at[0], ring_r.at[gslot(direction, step, j)])
            if step < H - 1 or (step == H - 1 and half == direction):
                onward(direction, step + 1, j, piece)

    def beginning(j):
        dy, half = order[j]
        piece = chunk(x, ya(-dy), half)
        k = dy * 2 + half
        got(piece, y_s.at[k], y_r.at[k])
        onward(0, 1, j, piece)
        onward(1, 1, j, piece)

    lead = 2 + len(beside)
    for j in range(2, lead):
        beginning(j)
    relay(1, 0)
    relay(1, 1)
    for j in range(lead, NJ):
        beginning(j)
    use(x)
    for step in range(1, H + 1):
        for j in range(NJ):
            if step > 1 or j > 1:
                relay(step, j)
        if step < H:
            use(xa(-step))
            use(xa(step))
            for k in range((step - 1) * X // (H - 1), step * X // (H - 1)):
                spread(k)
    use(xa(H))


    def doubled(v, half):
        turned = pltpu.roll(v, HR, 1)
        return jnp.where(lo, v, turned) if half == 0 else jnp.where(lo, turned, v)

    hidden = doubled(acc[pl.ds(0, CF), :], 0)
    back = doubled(acc[pl.ds(CF, CF), :], 1)
    logit = doubled(acc[pl.ds(2 * CF, 8), :], 0)[0:1]
    gating = 1.0 / (1.0 + jnp.exp(-logit))
    c0 = 0.7978845608028654
    c1 = 0.044715
    sq = hidden * hidden
    th = jnp.tanh(c0 * (hidden + c1 * (sq * hidden)))
    cdf = 0.5 * (1.0 + th)
    act = hidden * cdf
    slope = cdf + (0.5 * hidden) * (1.0 - th * th) * (c0 * (1.0 + (3.0 * c1) * sq))
    zero = jnp.zeros_like(hidden)
    pre = slope * (gating * back)
    pre_lo = jnp.where(lo, pre, zero).astype(BF)
    bd[pl.ds(0, CF), :] = pre_lo
    bd[pl.ds(CF, CF), :] = jnp.where(lo, zero, pre).astype(BF)

    def partial(d):
        xx = xa(d)
        at = pl.ds(pl.multiple_of(xx * PW, PW), PW)
        pf[xx] = dot(u2[:, at], bd[...], TN).reshape(Y, CW, R)

    ahead = sorted(range(Y), key=lambda d: -min(d, Y - d))

    def pass_on(direction, m, j, hops=1):
        to = (e, tid(xa(hops if direction == 0 else -hops), y, core))
        k = slot(direction, m, j)
        go(outb.at[k], inb.at[k], ch_s.at[0], ch_r.at[k], to, False)

    def came(direction, m, j):
        k = slot(direction, m, j)
        got(inb.at[k], ch_s.at[0], ch_r.at[k])
        return inb[k].astype(F32)

    partial(H)
    for j in range(Y):
        direction = 0 if j in halves[0] else 1
        outb[slot(direction, 1, j)] = pf[xa(H), ya(ahead[j])].astype(BF)
        pass_on(direction, 1, j, 2)

    l2[pl.ds(0, CF), :] = pre_lo
    l2[pl.ds(CF, CF), :] = jnp.where(lo, zero, act * gating).astype(BF)
    gp[...] = jnp.sum(act.astype(BF).astype(F32) * back, axis=0, keepdims=True)
    for dy in range(1, Y):
        go(gp, gy.at[dy], gy_s.at[dy], gy_r.at[dy], (e, tid(x, ya(dy), core)))
    def grads(k):
        at = pl.ds(k * SW, SW)
        gr[:, at] = dot(l2[...], xg[at, :], NT).astype(BF)

    done = 0
    for m in range(2, H + 1):
        if m == 2:
            partial(H - 1)
            partial(1 - H)
        if m == 3:
            for d in range(H - 2, 0, -1):
                partial(d)
                partial(-d)
            partial(0)
        for late in (True, False):
            for j in range(Y):
                for direction in range(2):
                    if (j in halves[direction]) != late:
                        continue
                    dest = xa((H + 1 - m) * (1 if direction == 0 else -1))
                    value = pf[dest, ya(ahead[j])]
                    if m == 3 and late:
                        value = value + came(direction, 1, j)
                    if m > 2:
                        value = value + came(direction, m - 1, j)
                    outb[slot(direction, m, j)] = value.astype(BF)
                    pass_on(direction, m, j)
        if m == 2:
            total = gp[...]
            for dy in range(1, Y):
                got(gy.at[dy], gy_s.at[dy], gy_r.at[dy])
                total = total + gy[dy]
            gs[...] = total
            for dx in range(1, X):
                go(gs, gx.at[dx], gx_s.at[dx], gx_r.at[dx], (e, tid(xa(dx), y, core)))
        for _ in range(X // (H - 1)):
            grads(done)
            done += 1
    while done < X:
        grads(done)
        done += 1
    outs = [
        pltpu.make_async_copy(gr.at[mine], ug_hbm.at[mine], osem.at[0]),
        pltpu.make_async_copy(gr.at[mine_dn], dg_hbm.at[mine], osem.at[1]),
    ]
    for copy in outs:
        copy.start()
    go(gr.at[his], ug_hbm.at[mine], g_s.at[0], g_r.at[0], sib)
    go(gr.at[his_dn], dg_hbm.at[mine], g_s.at[1], g_r.at[1], sib)

    gate_total = gs[...]
    for dx in range(1, X):
        got(gx.at[dx], gx_s.at[dx], gx_r.at[dx])
        gate_total = gate_total + gx[dx]
    slopes = gate_total * gating * (1.0 - gating)
    srow = lax.broadcasted_iota(jnp.int32, (KP, R), 0)
    one_row = jnp.where((srow == 0) & lo, slopes, 0.0)
    hi = one_row.astype(BF)
    rest = one_row - hi.astype(F32)
    mid = rest.astype(BF)
    low = (rest - mid.astype(F32)).astype(BF)

    def embed_part(tt):
        xs = xg[pl.ds(pl.multiple_of(tt * CW, CW), CW), :]
        return (dot(hi, xs, NT) + dot(mid, xs, NT) + dot(low, xs, NT))[0:8]

    ego[...] = jnp.concatenate(
        [embed_part(tid(x, y, other)), jnp.zeros((8, 128 - CW), F32)], axis=1
    )
    go(ego, egi, e_s.at[0], e_r.at[0], sib)
    own_part = embed_part(t)[0:1]
    outer = ec[...] * slopes
    for j in range(Y):
        dy = ahead[j]
        value = pf[x, ya(dy)] + came(0, H, j) + came(1, H, j)
        if dy:
            yo[dy] = value.astype(BF)
            go(yo.at[dy], yi.at[dy], yr_s.at[dy], yr_r.at[dy], (e, tid(x, ya(dy), core)))
        else:
            summed = value + outer
    n_half = (2 * H - 1) * Y
    gone(xg.at[pl.ds(0, n_half * CH)], ring_s.at[0], ring_r.at[0])
    gone(outb.at[pl.ds(0, n_half)], ch_s.at[0], ch_r.at[0])
    for dy in sorted(range(1, Y), key=lambda d: min(d, Y - d)):
        got(yi.at[dy], yr_s.at[dy], yr_r.at[dy])
        summed = summed + yi[dy].astype(F32)
    summed = summed.astype(BF)

    pad = jnp.zeros((NQ, 128 - CW), BF)
    for rel in (1, 0):
        to = core if rel == 0 else other
        block = dot(bh[to], summed, NT).astype(BF)
        sbuf2[pl.ds(to * NE, NE)] = jnp.concatenate([block, pad], axis=1).reshape(NE, KP, 128)
        for way, o in pairs:
            if way == rel:
                go(
                    sbuf2.at[to * NE + ea(o)], rbuf2.at[core * NE + e],
                    b_s.at[0], b_r.at[0], (ea(o), tid(x, y, to)), False,
                )
    rbuf2[core * NE + e] = sbuf2[core * NE + e]
    drain()
    got(egi, e_s.at[0], e_r.at[0])
    row2 = lax.broadcasted_iota(jnp.int32, (2, CW), 0)
    egv[...] = jnp.where(row2 == core, own_part, egi[...][0:1, :CW])
    outs.append(pltpu.make_async_copy(egv, eg_hbm, osem.at[2]))
    outs[-1].start()
    got(ug_hbm.at[his], g_s.at[0], g_r.at[0])
    got(dg_hbm.at[his], g_s.at[1], g_r.at[1])
    gone(sbuf2.at[pl.ds(0, 2 * NE - 1)], b_s.at[0], b_r.at[0])
    got(rbuf2.at[pl.ds(0, 2 * NE - 1)], b_s.at[0], b_r.at[0])
    placed = sum(
        dot(rbuf2[pl.ds(el * NE, NE)].reshape(NQ, 128)[:, :CW], otq[el], TN) for el in range(2)
    )
    tgv[...] = (both[pl.ds(CW, CW), :].astype(F32) + placed).astype(BF)
    outs.append(pltpu.make_async_copy(tgv, tg_hbm, osem.at[3]))
    outs[-1].start()
    for copy in outs:
        copy.wait()


def hand_over(*refs):
    ins, outs, held, sems = refs[:4], refs[4:8], refs[8:12], refs[12]
    places = [(i, pl.ds(r, CUT)) for r in range(0, ins[1].shape[0], CUT) for i in (1, 2)]
    places += [(0, pl.ds(0, ins[0].shape[0])), (3, pl.ds(0, ins[3].shape[0]))]
    n = len(places)
    first, second = [], []
    for k, (i, at) in enumerate(places):
        first.append(pltpu.make_async_copy(ins[i].at[at], held[i].at[at], sems.at[k]))
        second.append(pltpu.make_async_copy(held[i].at[at], outs[i].at[at], sems.at[n + k]))
        first[k].start()
    for k in range(n):
        first[k].wait()
        second[k].start()
    for copy in second:
        copy.wait()


def local(groups, tensors, tokens, cotangent, routing, up_weight, down_weight, expert_embed):
    rows, cw = tokens.shape
    el, depth, fl = up_weight.shape
    sl = rows // (groups * el)
    xs = tensors // (2 * Y)
    dims = (groups, sl, cw, xs, fl)
    h = xs // 2
    cf = 2 * fl
    vm = pltpu.VMEM
    dma = pltpu.SemaphoreType.DMA
    n_ring = 2 * (h + 1) * Y

    def pair(n):
        return [dma((n,)), dma((n,))]

    scratch = [
        vm((2 * cw, rows), BF),
        vm((1, rows), jnp.int32),
        vm((el, depth), BF),
        vm((rows, rows), BF),
        vm((2, groups * KP, rows), BF),
        vm((2, groups * KP, rows), BF),
        vm((cw, rows), F32),
        vm((2 * groups, KP, 2 * cw + 64), BF),
        vm((2 * groups, KP, 2 * cw + 64), BF),
        vm((depth, rows), BF),
        vm((2 * cf + KP, depth), BF),
        vm((2 * cf, depth // 2), BF),
        vm((2 * cf + KP, rows), F32),
        vm((2 * cf, rows), BF),
        vm((2 * cf, rows), BF),
        vm((2 * cf, depth), BF),
        vm((xs, Y, cw, rows), F32),
        vm((2 * (h + 1) * Y, cw, rows), BF),
        vm((2 * (h + 1) * Y, cw, rows), BF),
        vm((Y, cw, rows), BF),
        vm((Y, cw, rows), BF),
        vm((1, rows), F32),
        vm((Y, 1, rows), F32),
        vm((1, rows), F32),
        vm((xs, 1, rows), F32),
        vm((8, 128), F32),
        vm((8, 128), F32),
        vm((el, cw), F32),
        vm((cw, rows), BF),
        vm((2 * groups, KP, 128), BF),
        vm((2 * groups, KP, 128), BF),
        dma((6,)),
        dma((4,)),
        *pair(2),
        *pair(1),
        *pair(2 * Y),
        dma((1,)), dma((2 * n_ring,)),
        dma((1,)), dma((n_ring,)),
        *pair(Y),
        *pair(Y),
        *pair(xs),
        *pair(2),
        *pair(1),
        *pair(1),
    ]
    hbm = pl.BlockSpec(memory_space=pl.ANY)
    shapes = (
        jax.ShapeDtypeStruct((cw, rows), BF),
        jax.ShapeDtypeStruct((el * fl, depth), BF),
        jax.ShapeDtypeStruct((el * fl, depth), BF),
        jax.ShapeDtypeStruct((el, cw), F32),
    )
    made = pl.pallas_call(
        functools.partial(kernel, dims),
        out_shape=shapes,
        in_specs=[hbm] * 6,
        out_specs=(hbm,) * 4,
        scratch_shapes=scratch,
        compiler_params=pltpu.CompilerParams(
            collective_id=0, has_side_effects=True, vmem_limit_bytes=60 * 1024 * 1024
        ),
    )(
        tokens.T,
        cotangent.T,
        routing,
        up_weight.transpose(0, 2, 1).reshape(el * fl, depth),
        down_weight.reshape(el * fl, depth),
        expert_embed,
    )
    tg, ug, dg, eg = pl.pallas_call(
        hand_over,
        out_shape=shapes,
        in_specs=[hbm] * 4,
        out_specs=(hbm,) * 4,
        scratch_shapes=[vm(shape.shape, shape.dtype) for shape in shapes] + [dma((4 * (el * fl // CUT) + 4,))],
        compiler_params=pltpu.CompilerParams(vmem_limit_bytes=60 * 1024 * 1024),
    )(*made)
    return (
        tg.T,
        ug.reshape(el, fl, depth).transpose(0, 2, 1),
        dg.reshape(el, fl, depth),
        eg,
    )


def solution(mesh):
    return jax.shard_map(
        functools.partial(local, mesh.shape["expert"], mesh.shape["tensor"]),
        mesh=mesh,
        in_specs=(
            P("expert", "tensor"),
            P("expert", "tensor"),
            P("expert", None),
            P("expert", None, "tensor"),
            P("expert", "tensor", None),
            P("expert", None),
        ),
        out_specs=(
            P("expert", "tensor"),
            P("expert", None, "tensor"),
            P("expert", "tensor", None),
            P("expert", "tensor"),
        ),
        check_vma=False,
    )
```
